512 devices in a mesh: row: 16 (over y, x), col: 32 (over z, core).
Axes of the slice: x: 4, y: 4, z: 16, core: 2. Of those that a mesh axis runs over, the one named last changes fastest.
Arguments:
- features: bfloat16 [65536, 128], P(('col', 'row')), may hold values from -6 to 6
- tiles: bfloat16 [16, 32, 16, 128, 128], P('row', 'col'), may hold values from -0.25 to 0.25
- tile_rows: int32 [16, 32, 16], P('row', 'col'), may hold values from 0 to 31, as said below
- tile_cols: int32 [16, 32, 16], P('row', 'col'), may hold values from 0 to 15, as said below
- tile_count: int32 [16, 32], P('row', 'col'), may hold values from 2 to 16, as said below
- weight: float32 [128, 256], replicated, may hold values from -0.5 to 0.5
- bias: float32 [256], replicated, may hold values from -3 to 3
- cotangent: bfloat16 [65536, 256], P(('row', 'col')), may hold values from -6 to 6
Outputs:
- output: bfloat16 [65536, 256], P(('row', 'col'))
- grad_features: bfloat16 [65536, 128], P(('col', 'row'))
- grad_weight: float32 [128, 256], replicated
- grad_bias: float32 [256], replicated
The draws below stay inside these ranges and needn't reach their ends.
Inputs may be any that keep to these rules, and one draw needn't show every extreme that they name: `tile_rows`: within one device the live slots name distinct tile places; dead slots hold values that are not part of A. `tile_cols`: distinct places within one device, together with tile_rows. `tile_count`: some device has all 16 slots live.
All inputs are finite; a program needn't handle non-finite values.
Results may differ from the reference program's by a relative error of at most 0.023.
Values may be sent and summed in bfloat16 or wider, within the bound.
A program may use at most 128 MiB of HBM per device.

```python
import jax
import jax.numpy as jnp
from jax import lax

TILE = 128
F = 128
HID = 256
BR = 32
K_DEV = 16
BC = 16
NODES = 65536
N_ROW = 16
N_COL = 32


def tile_slots(key):
    keys = jax.random.split(key, N_ROW * N_COL)
    picks = jax.vmap(lambda single: jax.random.permutation(single, BR * BC)[:K_DEV])(keys)
    return picks.reshape(N_ROW, N_COL, K_DEV).astype(jnp.int32)


def draw_tile_rows(key, part):
    return (tile_slots(key) // BC).astype(jnp.int32)


def draw_tile_cols(key, part):
    return (tile_slots(key) % BC).astype(jnp.int32)


def draw_tile_count(key, part):
    key = jax.random.fold_in(key, 7)
    first, second = jax.random.split(key)
    level = jax.random.randint(first, (N_ROW, N_COL), 0, 8)
    counts = jnp.maximum(max(1, K_DEV // 8), K_DEV * level * level // 64)
    chosen = jax.random.randint(second, (), 0, N_ROW * N_COL)
    places = jnp.arange(N_ROW * N_COL).reshape(N_ROW, N_COL)
    counts = jnp.where(places == chosen, K_DEV, counts)
    return counts.astype(jnp.int32)


def steps_of(rng, dims, shards, least, largest):
    def one(axis_at, blocks):
        steps = jax.random.uniform(jax.random.fold_in(jax.random.fold_in(rng, 6), axis_at), (blocks,), jnp.float32, least / len(shards), largest / len(shards))
        return jnp.repeat(jnp.exp(steps), dims[axis_at] // blocks).reshape((-1,) + (1,) * (len(dims) - axis_at - 1))

    level = one(*shards[0])
    for cut in shards[1:]:
        level = level * one(*cut)
    return level


def scatter_about(key, extent, scale, limit, cuts=(), dtype=jnp.bfloat16):
    result = scale * jax.random.normal(key, extent, jnp.float32)
    if cuts:
        result = result * steps_of(key, extent, cuts, -0.22, 0.18)
    return jnp.clip(result, -limit, limit).astype(dtype)


def setup_inputs(seed: int = 0) -> dict:
    key_of = jax.random.split(jax.random.key(seed), 9)
    features = scatter_about(key_of[0], (NODES, F), 1.0, 6.0, ((0, 512),))
    tiles = scatter_about(key_of[1], (N_ROW, N_COL, K_DEV, TILE, TILE), (4 * TILE) ** -0.5, 0.25, ((0, 16), (1, 32)))
    tile_rows = draw_tile_rows(jax.random.fold_in(key_of[8], 71), 0)
    tile_cols = draw_tile_cols(jax.random.fold_in(key_of[8], 71), 0)
    tile_count = draw_tile_count(jax.random.fold_in(key_of[8], 71), 0)
    weight = scatter_about(key_of[5], (F, HID), F ** -0.5, 0.5, (), jnp.float32)
    bias = scatter_about(key_of[6], (HID,), 0.5, 3.0, (), jnp.float32)
    cotangent = scatter_about(key_of[7], (NODES, HID), 1.0, 6.0, ((0, 512),))
    return dict(features=features, tiles=tiles, tile_rows=tile_rows, tile_cols=tile_cols, tile_count=tile_count, weight=weight, bias=bias, cotangent=cotangent)


def reference(features, tiles, tile_rows, tile_cols, tile_count, weight, bias, cotangent):
    size = tiles.shape[3]
    width = features.shape[1]
    nrow = tiles.shape[0]
    ncol = tiles.shape[1]
    slots = jnp.arange(tiles.shape[2])
    high = lax.Precision.HIGHEST

    def forward_block(rindex):

        def add_col(total, cindex):
            blocks = tiles[rindex, cindex].astype(jnp.float32)
            source = lax.dynamic_slice_in_dim(features, (cindex * BC * size).astype(jnp.int32), BC * size, 0)
            picked = source.reshape(BC, size, width).astype(jnp.float32)[tile_cols[rindex, cindex]]
            products = jnp.einsum('kij,kjf->kif', blocks, picked)
            live = (slots < tile_count[rindex, cindex]).astype(jnp.float32)
            onehot = (tile_rows[rindex, cindex][:, None] == jnp.arange(BR)[None, :]).astype(jnp.float32) * live[:, None]
            partial_value = jnp.einsum('kb,kif->bif', onehot, products, precision=high)
            rounded = lax.optimization_barrier(partial_value.astype(jnp.bfloat16))
            return (total + rounded.astype(jnp.float32), None)
        total, unused = lax.scan(add_col, jnp.zeros((BR, size, width), jnp.float32), jnp.arange(ncol))
        return total
    aggregated = lax.map(forward_block, jnp.arange(nrow)).reshape(-1, width).astype(jnp.bfloat16)
    pre = jnp.dot(aggregated.astype(jnp.float32), weight, precision=high) + bias
    value, act_vjp = jax.vjp(jax.nn.gelu, pre)
    output = value.astype(jnp.bfloat16)
    dpre = act_vjp(cotangent.astype(jnp.float32))[0]
    grad_weight = jnp.dot(aggregated.astype(jnp.float32).T, dpre, precision=high)
    grad_bias = lax.optimization_barrier(jnp.sum(dpre, axis=0))
    daggregated = jnp.dot(dpre, weight.T, precision=high).astype(jnp.bfloat16)

    def backward_block(cindex):

        def add_row(total, rindex):
            blocks = tiles[rindex, cindex].astype(jnp.float32)
            source = lax.dynamic_slice_in_dim(daggregated, (rindex * BR * size).astype(jnp.int32), BR * size, 0)
            picked = source.reshape(BR, size, width).astype(jnp.float32)[tile_rows[rindex, cindex]]
            products = jnp.einsum('kji,kjf->kif', blocks, picked)
            live = (slots < tile_count[rindex, cindex]).astype(jnp.float32)
            onehot = (tile_cols[rindex, cindex][:, None] == jnp.arange(BC)[None, :]).astype(jnp.float32) * live[:, None]
            partial_value = jnp.einsum('kb,kif->bif', onehot, products, precision=high)
            rounded = lax.optimization_barrier(partial_value.astype(jnp.bfloat16))
            return (total + rounded.astype(jnp.float32), None)
        total, unused = lax.scan(add_row, jnp.zeros((BC, size, width), jnp.float32), jnp.arange(nrow))
        return total
    grad_features = lax.map(backward_block, jnp.arange(ncol)).reshape(-1, width).astype(jnp.bfloat16)
    return (output, grad_features, grad_weight, grad_bias)
```

```python
import jax
import jax.numpy as jnp
from jax import lax
from jax.experimental import pallas as pl
from jax.experimental.pallas import tpu as pltpu
from jax.sharding import PartitionSpec as P

MESH = pl.DeviceIdType.MESH
F32 = jnp.float32
BF16 = jnp.bfloat16
T = 128
K = 16
NX = 4
NY = 4
NZ = 16
NP = NX * NY
BR = 32
NODES = 65536
HID = 256
LEAF = {5: 6, 7: 6, 8: 6, -4: -5, -6: -5, -7: -5, 2: 3, 4: 3, -3: -2}
RELAY = [6, -5, 3, -2]
NEAR = [1, -1]
ORDER = list(LEAF) + NEAR + RELAY + [0]
AT = {p: n for n, p in enumerate(ORDER)}
C0 = 0.7978845608028654
C1 = 0.044715


def dot(a, b, dims=((1,), (0,))):
    return lax.dot_general(a, b, (dims, ((), ())), preferred_element_type=F32)


def split(v):
    hi = v.astype(BF16)
    return hi, (v - hi.astype(F32)).astype(BF16)


def kernel(
    feat, tiles_hbm, rows, cols, count, w_hbm, bias, cot_hbm,
    out, gf, gw, gb,
    tiles, w, cot, feats, sums, part, sib, bsend, brecv, dagg, qpart, qrecv,
    epart, erecv, ehalf, esib, zmine, zrecv, fin, gwrecv,
    in_sem, a_ss, a_rs, p_ss, p_rs, b_ss, b_rs,
    c_ss, c_rs, cs_ss, cs_rs, q_ss, q_rs,
    e_ss, e_rs, es_ss, es_rs, z_ss, z_rs, g_ss, g_rs,
):
    r = lax.axis_index("row")
    c = lax.axis_index("col")
    y, x = r // NX, r % NX
    z, core = c // 2, c % 2

    def plane(i):
        return ((y + i // NX) % NY) * NX + (x + i % NX) % NX

    def ring(i):
        return ((z + i) % NZ) * 2 + core

    me_other = (r, z * 2 + 1 - core)
    loads = [
        pltpu.make_async_copy(a, b, in_sem.at[n])
        for n, (a, b) in enumerate(
            ((feat, feats.at[r]), (tiles_hbm, tiles), (w_hbm, w), (cot_hbm, cot))
        )
    ]
    for copy in loads:
        copy.start()
    started = []

    def send(src, dst, ssem, rsem, where):
        copy = pltpu.make_async_remote_copy(
            src_ref=src, dst_ref=dst, send_sem=ssem, recv_sem=rsem,
            device_id=where, device_id_type=MESH,
        )
        copy.start()
        started.append(copy)
        return copy

    barrier = pltpu.get_barrier_semaphore()
    for i in range(1, NP):
        pl.semaphore_signal(barrier, inc=1, device_id=(plane(i), c), device_id_type=MESH)
    for i in range(1, NZ):
        pl.semaphore_signal(barrier, inc=1, device_id=(r, ring(i)), device_id_type=MESH)
    pl.semaphore_signal(barrier, inc=1, device_id=me_other, device_id_type=MESH)
    pl.semaphore_wait(barrier, NP + NZ - 1)

    a_copies = [
        send(feat, feats.at[r], a_ss.at[i], a_rs.at[i], (plane(i), c))
        for i in range(1, NP)
    ]

    live = count[0]
    dead = [NODES * jnp.minimum(jnp.maximum(k + 1 - live, 0), 1) for k in range(K)]
    slot_r = [rows[k] + dead[k] for k in range(K)]
    slot_c = [cols[k] + dead[k] for k in range(K)]

    def latest(slots, n, b):
        found = jnp.int32(0)
        for k in range(n):
            apart = slots[k] - b
            differs = jnp.minimum(jnp.maximum(apart, -apart), 1)
            found = jnp.maximum(found, (k + 1) * (1 - differs))
        return found

    prev_r = [latest(slot_r, k, slot_r[k]) for k in range(K)]
    prev_c = [latest(slot_c, k, slot_c[k]) for k in range(K)]
    last_r = [
        [latest(slot_r, K, ring(NZ - p) // 2 * 2 + half) for p in ORDER]
        for half in (1 - core, core)
    ]
    last_c = [latest(slot_c, K, plane(i)) for i in range(NP)]

    sums[0] = jnp.zeros((T, T), F32)
    for copy in loads:
        copy.wait()
    for copy in a_copies:
        copy.wait_recv()

    for k in range(K):
        sums[k + 1] = dot(tiles[k], feats[jnp.minimum(jnp.maximum(cols[k], 0), NP - 1)])
    for k in range(1, K):
        sums[k + 1] = sums[k + 1] + sums[prev_r[k]]

    p_copies = []
    for g in range(4):
        for j in range(4 * g, 4 * g + 4):
            part[0, j] = sums[last_r[0][j]].astype(BF16)
        four = pl.ds(4 * g, 4)
        p_copies.append(
            send(part.at[0, four], sib.at[four], p_ss.at[g], p_rs.at[g], me_other)
        )
    for j in range(NZ):
        part[1, j] = sums[last_r[1][j]].astype(BF16)

    b_copies = {}

    def own(p):
        j = AT[p]
        if j % 4 == 0:
            p_copies[j // 4].wait_recv()
        return part[1, j].astype(F32) + sib[j].astype(F32)

    def pass_on(p, to):
        v = own(p)
        for leaf, relay in LEAF.items():
            if relay == p:
                b_copies[leaf].wait_recv()
                v = v + brecv[AT[leaf]].astype(F32)
        n = AT[p]
        bsend[n] = v.astype(BF16)
        b_copies[p] = send(
            bsend.at[n], brecv.at[n], b_ss.at[n], b_rs.at[n], (r, ring(NZ + to - p))
        )

    for p in ORDER[:-1]:
        pass_on(p, LEAF.get(p, 0))
    total = own(0)
    for p in NEAR + RELAY:
        b_copies[p].wait_recv()
        total = total + brecv[AT[p]].astype(F32)
    agg = total.astype(BF16)

    w_hi, w_lo = split(w[...])
    pre = dot(agg, w_hi) + dot(agg, w_lo) + bias[...]
    square = pre * pre
    t = jnp.tanh(C0 * (pre + C1 * (square * pre)))
    half = 0.5 * (1.0 + t)
    slope = half + 0.5 * pre * (1.0 - t * t) * (C0 * (1.0 + 3.0 * C1 * square))
    dpre = cot[...].astype(F32) * slope
    dp_hi, dp_lo = split(dpre)
    back = ((1,), (1,))
    da = dot(dp_hi, w_hi, back) + dot(dp_lo, w_hi, back) + dot(dp_hi, w_lo, back)
    dagg[c] = da.astype(BF16)

    c_copies = {}

    def c_send(p, via):
        block = dagg.at[ring(NZ - via)]
        n = AT[p]
        c_copies[p] = send(
            block, block, c_ss.at[n], c_rs.at[n], (r, ring(NZ + p - via))
        )

    cs_copies = []

    def c_share(p):
        block = dagg.at[ring(NZ - p)]
        n = AT[p]
        cs_copies.append(send(block, block, cs_ss.at[n], cs_rs.at[n], me_other))

    for p in RELAY + NEAR:
        c_send(p, 0)
    c_share(0)

    out[...] = (pre * half).astype(BF16)
    down0 = ((0,), (0,))
    local_w = dot(agg, dp_hi, down0) + dot(agg, dp_lo, down0)
    local_b = jnp.sum(dpre.reshape(T // 8, 8, HID), axis=0)
    for p in range(NP):
        epart[p, 0:8] = local_w[8 * p : 8 * p + 8]
        epart[p, 8:16] = local_b
    e_copies = [
        send(epart.at[plane(i)], erecv.at[i], e_ss.at[i], e_rs.at[i], (plane(i), c))
        for i in range(1, NP)
    ]

    for via in RELAY:
        c_copies[via].wait_recv()
        for p, relay in LEAF.items():
            if relay == via:
                c_send(p, via)
        c_share(via)
    for p in NEAR:
        c_copies[p].wait_recv()
        c_share(p)

    acc = epart[r]
    for i in range(1, NP):
        e_copies[i - 1].wait_recv()
        acc = acc + erecv[i]
    ehalf[...] = acc
    other = pl.ds(pl.multiple_of((1 - core) * 8, 8), 8)
    es_copy = send(ehalf.at[other], esib.at[0], es_ss.at[0], es_rs.at[0], me_other)

    for p in LEAF:
        c_copies[p].wait_recv()
        c_share(p)
    es_copy.wait_recv()
    keep = pl.ds(pl.multiple_of(core * 8, 8), 8)
    zmine[...] = ehalf[keep, :] + esib[0]
    z_copies = [
        send(zmine, zrecv.at[i], z_ss.at[i], z_rs.at[i], (r, ring(i)))
        for i in range(1, NZ)
    ]
    for copy in cs_copies:
        copy.wait_recv()

    for k in range(K):
        picked = dagg[jnp.minimum(jnp.maximum(rows[k], 0), BR - 1)]
        sums[k + 1] = dot(tiles[k], picked, down0)
    for k in range(1, K):
        sums[k + 1] = sums[k + 1] + sums[prev_c[k]]
    q_copies = []
    for i in range(NP):
        qpart[i] = sums[last_c[i]].astype(BF16)
        if i:
            q_copies.append(send(qpart.at[i], qrecv.at[i], q_ss.at[i], q_rs.at[i], (plane(i), c)))

    acc = zmine[...]
    for i in range(1, NZ):
        z_copies[i - 1].wait_recv()
        acc = acc + zrecv[i]
    fin[core] = acc
    share = send(fin.at[core], fin.at[core], es_ss.at[1], es_rs.at[1], me_other)
    share.wait_recv()
    g_copies = [
        send(fin.at[0], gwrecv.at[r], g_ss.at[i], g_rs.at[i], (plane(i), c))
        for i in range(1, NP)
    ]
    gwrecv[r] = fin[0]
    gb[...] = jnp.sum(fin[1], axis=0, keepdims=True)

    acc = qpart[0].astype(F32)
    for i in range(1, NP):
        q_copies[i - 1].wait_recv()
        acc = acc + qrecv[i].astype(F32)
    gf[...] = acc.astype(BF16)
    for copy in g_copies:
        copy.wait_recv()
    for p in range(NP):
        gw[8 * p : 8 * p + 8, :] = gwrecv[p]
    for copy in started:
        copy.wait_send()


def on_device(features, tiles, tile_rows, tile_cols, tile_count, weight, bias, cotangent):
    vmem = pl.BlockSpec(memory_space=pltpu.VMEM)
    smem = pl.BlockSpec(memory_space=pltpu.SMEM)
    hbm = pl.BlockSpec(memory_space=pl.ANY)
    dma = pltpu.SemaphoreType.DMA
    out, gf, gw, gb = pl.pallas_call(
        kernel,
        out_shape=(
            jax.ShapeDtypeStruct((T, HID), BF16),
            jax.ShapeDtypeStruct((T, T), BF16),
            jax.ShapeDtypeStruct((T, HID), F32),
            jax.ShapeDtypeStruct((1, HID), F32),
        ),
        in_specs=[hbm, hbm, smem, smem, smem, hbm, vmem, hbm],
        out_specs=(vmem,) * 4,
        scratch_shapes=[
            pltpu.VMEM((K, T, T), BF16),
            pltpu.VMEM((T, HID), F32),
            pltpu.VMEM((T, HID), BF16),
            pltpu.VMEM((NP, T, T), BF16),
            pltpu.VMEM((K + 1, T, T), F32),
            pltpu.VMEM((2, NZ, T, T), BF16),
            pltpu.VMEM((NZ, T, T), BF16),
            pltpu.VMEM((NZ, T, T), BF16),
            pltpu.VMEM((NZ, T, T), BF16),
            pltpu.VMEM((2 * NZ, T, T), BF16),
            pltpu.VMEM((NP, T, T), BF16),
            pltpu.VMEM((NP, T, T), BF16),
            pltpu.VMEM((NP, 16, HID), F32),
            pltpu.VMEM((NP, 16, HID), F32),
            pltpu.VMEM((16, HID), F32),
            pltpu.VMEM((1, 8, HID), F32),
            pltpu.VMEM((8, HID), F32),
            pltpu.VMEM((NZ, 8, HID), F32),
            pltpu.VMEM((2, 8, HID), F32),
            pltpu.VMEM((NP, 8, HID), F32),
            dma((4,)),
        ]
        + [dma((16,))] * 20,
        compiler_params=pltpu.CompilerParams(
            collective_id=0, has_side_effects=True, vmem_limit_bytes=60 * 1024 * 1024
        ),
    )(
        features,
        tiles.reshape(K, T, T),
        tile_rows.reshape(K),
        tile_cols.reshape(K),
        tile_count.reshape(1),
        weight,
        bias.reshape(1, HID),
        cotangent,
    )
    return out, gf, gw, gb.reshape(HID)


def solution(mesh):
    placed = (
        P(("col", "row"), None),
        P("row", "col", None, None, None),
        P("row", "col", None),
        P("row", "col", None),
        P("row", "col"),
        P(),
        P(),
        P(("row", "col"), None),
    )
    return jax.shard_map(
        on_device,
        mesh=mesh,
        in_specs=placed,
        out_specs=(P(("row", "col"), None), P(("col", "row"), None), P(), P()),
        check_vma=False,
    )
```

```python
import jax
import jax.numpy as jnp
from jax import lax
from jax.experimental import pallas as pl
from jax.experimental.pallas import tpu as pltpu
from jax.sharding import PartitionSpec as P

MESH = pl.DeviceIdType.MESH
F32 = jnp.float32
BF16 = jnp.bfloat16
T = 128
K = 16
NX = 4
NY = 4
NZ = 16
NP = NX * NY
BR = 32
NODES = 65536
HID = 256
LEAF = {5: 6, 7: 6, 8: 6, -4: -5, -6: -5, -7: -5, 2: 3, 4: 3, -3: -2}
RELAY = [6, -5, 3, -2]
NEAR = [1, -1]
ORDER = list(LEAF) + NEAR + RELAY + [0]
FAR_FIRST = sorted(range(1, NP), key=lambda i: -min(i // 4, 4 - i // 4) - min(i % 4, 4 - i % 4))
AT = {p: n for n, p in enumerate(ORDER)}
C0 = 0.7978845608028654
C1 = 0.044715


def dot(a, b, dims=((1,), (0,))):
    return lax.dot_general(a, b, (dims, ((), ())), preferred_element_type=F32)


def split(v):
    hi = v.astype(BF16)
    return hi, (v - hi.astype(F32)).astype(BF16)


def kernel(
    feat, tiles_hbm, rows_hbm, cols_hbm, count_hbm, w_hbm, bias_hbm, cot_hbm,
    out, gf, gw, gb,
    rows, cols, count, tiles, w, bias, cot, feats, sums, part, sib, bsend, brecv, dagg, qpart, qrecv,
    epart, erecv, zall, fin,
    in_sem, a_ss, a_rs, p_ss, p_rs, b_ss, b_rs,
    c_ss, c_rs, cs_ss, cs_rs, q_ss, q_rs,
    e_ss, e_rs, z_ss, z_rs, g_ss, g_rs,
):
    r = lax.axis_index("row")
    c = lax.axis_index("col")
    y, x = r // NX, r % NX
    z, core = c // 2, c % 2

    def plane(i):
        return ((y + i // NX) % NY) * NX + (x + i % NX) % NX

    def ring(i):
        return ((z + i) % NZ) * 2 + core

    me_other = (r, z * 2 + 1 - core)
    operands = (
        (feat, feats.at[r]), (rows_hbm, rows), (cols_hbm, cols), (count_hbm, count),
        (tiles_hbm, tiles), (w_hbm, w), (bias_hbm, bias), (cot_hbm, cot),
    )
    loads = [pltpu.make_async_copy(a, b, in_sem.at[n]) for n, (a, b) in enumerate(operands)]
    for copy in loads:
        copy.start()
    started = []

    def send(src, dst, ssem, rsem, where):
        copy = pltpu.make_async_remote_copy(
            src_ref=src, dst_ref=dst, send_sem=ssem, recv_sem=rsem,
            device_id=where, device_id_type=MESH,
        )
        copy.start()
        started.append(copy)
        return copy

    barrier = pltpu.get_barrier_semaphore()
    for i in range(1, NP):
        pl.semaphore_signal(barrier, inc=1, device_id=(plane(i), c), device_id_type=MESH)
    for i in range(1, NZ):
        pl.semaphore_signal(barrier, inc=1, device_id=(r, ring(i)), device_id_type=MESH)
    pl.semaphore_signal(barrier, inc=1, device_id=me_other, device_id_type=MESH)
    pl.semaphore_wait(barrier, NP + NZ - 1)

    a_copies = [
        send(feat, feats.at[r], a_ss.at[i], a_rs.at[i], (plane(i), c)) for i in FAR_FIRST
    ]

    for copy in loads[1:4]:
        copy.wait()
    live = count[0]
    dead = [NODES * jnp.minimum(jnp.maximum(k + 1 - live, 0), 1) for k in range(K)]
    slot_r = [rows[k] + dead[k] for k in range(K)]
    slot_c = [cols[k] + dead[k] for k in range(K)]

    def latest(slots, n, b):
        found = jnp.int32(0)
        for k in range(n):
            apart = slots[k] - b
            differs = jnp.minimum(jnp.maximum(apart, -apart), 1)
            found = jnp.maximum(found, (k + 1) * (1 - differs))
        return found

    prev_r = [latest(slot_r, k, slot_r[k]) for k in range(K)]
    prev_c = [latest(slot_c, k, slot_c[k]) for k in range(K)]
    last_r = [
        [latest(slot_r, K, ring(NZ - p) // 2 * 2 + half) for p in ORDER]
        for half in (1 - core, core)
    ]
    last_c = [latest(slot_c, K, plane(i)) for i in range(NP)]

    sums[0] = jnp.zeros((T, T), F32)
    for copy in (loads[0], *loads[4:]):
        copy.wait()
    for copy in a_copies:
        copy.wait_recv()

    for k in range(K):
        sums[k + 1] = dot(tiles[k], feats[jnp.minimum(jnp.maximum(cols[k], 0), NP - 1)])
    for k in range(1, K):
        sums[k + 1] = sums[k + 1] + sums[prev_r[k]]

    p_copies = []
    for g in range(4):
        for j in range(4 * g, 4 * g + 4):
            part[j] = sums[last_r[0][j]].astype(BF16)
        four = pl.ds(4 * g, 4)
        p_copies.append(
            send(part.at[four], sib.at[four], p_ss.at[g], p_rs.at[g], me_other)
        )

    b_copies = {}

    def own(p):
        j = AT[p]
        if j % 4 == 0:
            p_copies[j // 4].wait_recv()
        return sums[last_r[1][j]] + sib[j].astype(F32)

    def pass_on(p, to):
        v = own(p)
        for leaf, relay in LEAF.items():
            if relay == p:
                b_copies[leaf].wait_recv()
                v = v + brecv[AT[leaf]].astype(F32)
        n = AT[p]
        bsend[n] = v.astype(BF16)
        b_copies[p] = send(
            bsend.at[n], brecv.at[n], b_ss.at[n], b_rs.at[n], (r, ring(NZ + to - p))
        )

    for p in ORDER[:-1]:
        pass_on(p, LEAF.get(p, 0))
    total = own(0)
    for p in NEAR + RELAY:
        b_copies[p].wait_recv()
        total = total + brecv[AT[p]].astype(F32)
    agg = total.astype(BF16)

    w_hi, w_lo = split(w[...])
    pre = dot(agg, w_hi) + dot(agg, w_lo) + bias[...]
    square = pre * pre
    t = jnp.tanh(C0 * (pre + C1 * (square * pre)))
    half = 0.5 * (1.0 + t)
    slope = half + 0.5 * pre * (1.0 - t * t) * (C0 * (1.0 + 3.0 * C1 * square))
    dpre = cot[...].astype(F32) * slope
    dp_hi, dp_lo = split(dpre)
    back = ((1,), (1,))
    da = dot(dp_hi, w_hi, back) + dot(dp_lo, w_hi, back) + dot(dp_hi, w_lo, back)
    dagg[c] = da.astype(BF16)

    c_copies = {}

    def c_send(p, via):
        block = dagg.at[ring(NZ - via)]
        n = AT[p]
        c_copies[p] = send(
            block, block, c_ss.at[n], c_rs.at[n], (r, ring(NZ + p - via))
        )

    cs_copies = []

    def c_share(p):
        block = dagg.at[ring(NZ - p)]
        n = AT[p]
        cs_copies.append(send(block, block, cs_ss.at[n], cs_rs.at[n], me_other))

    for p in RELAY + NEAR:
        c_send(p, 0)
    c_share(0)

    out[...] = (pre * half).astype(BF16)
    down0 = ((0,), (0,))
    local_w = dot(agg, dp_hi, down0) + dot(agg, dp_lo, down0)
    local_b = jnp.sum(dpre.reshape(T // 8, 8, HID), axis=0)
    for h in range(2):
        lanes = slice(T * h, T * h + T)
        for p in range(NP):
            epart[p, h, 0:8] = local_w[8 * p : 8 * p + 8, lanes]
            epart[p, h, 8:16] = local_b[:, lanes]

    cores = (core, 1 - core)
    pairs = [(i, t) for i in FAR_FIRST + [0] for t in (0, 1) if i or t]
    e_copies = [
        send(
            epart.at[plane(i), cores[t]], erecv.at[2 * i + t], e_ss.at[2 * i + t],
            e_rs.at[2 * i + t], (plane(i), z * 2 + cores[t]),
        )
        for i, t in pairs
    ]

    for via in RELAY:
        c_copies[via].wait_recv()
        for p, relay in LEAF.items():
            if relay == via:
                c_send(p, via)
        c_share(via)
    for p in NEAR:
        c_copies[p].wait_recv()
        c_share(p)

    for copy in e_copies:
        copy.wait_recv()
    acc = epart[r, core]
    for n in range(1, 2 * NP):
        acc = acc + erecv[n]
    zall[z] = acc.astype(BF16)
    z_copies = [
        send(zall.at[z], zall.at[z], z_ss.at[i], z_rs.at[i], (r, ring(i)))
        for i in (8, 7, 9, 6, 10, 5, 11, 4, 12, 3, 13, 2, 14, 1, 15)
    ]

    for p in LEAF:
        c_copies[p].wait_recv()
        c_share(p)
    for copy in cs_copies:
        copy.wait_recv()

    for k in range(K):
        picked = dagg[jnp.minimum(jnp.maximum(rows[k], 0), BR - 1)]
        sums[k + 1] = dot(tiles[k], picked, down0)
    for k in range(1, K):
        sums[k + 1] = sums[k + 1] + sums[prev_c[k]]
    q_copies = {}
    for i in FAR_FIRST + [0]:
        qpart[i] = sums[last_c[i]].astype(BF16)
        if i:
            q_copies[i] = send(
                qpart.at[i], qrecv.at[i], q_ss.at[i], q_rs.at[i], (plane(i), c)
            )
    early = len(started) - NP + 1
    for copy in started[:early]:
        copy.wait_send()

    for copy in z_copies:
        copy.wait_recv()
    acc = zall[0].astype(F32)
    for i in range(1, NZ):
        acc = acc + zall[i].astype(F32)
    fin[r, core] = acc
    g_copies = []
    for i, t in pairs:
        piece = fin.at[r, core, pl.ds(0, 8)] if i else fin.at[r, core]
        g_copies.append(
            send(piece, piece, g_ss.at[2 * i + t], g_rs.at[2 * i + t], (plane(i), z * 2 + cores[t]))
        )

    acc = qpart[0].astype(F32)
    for i in FAR_FIRST:
        q_copies[i].wait_recv()
        acc = acc + qrecv[i].astype(F32)
    gf[...] = acc.astype(BF16)
    for copy in g_copies:
        copy.wait_recv()
    for h in range(2):
        lanes = slice(T * h, T * h + T)
        for p in range(NP):
            gw[8 * p : 8 * p + 8, lanes] = fin[p, h, 0:8]
        gb[:, lanes] = jnp.sum(fin[r, h, 8:16], axis=0, keepdims=True)
    for copy in started[early:]:
        copy.wait_send()


def write_out(*refs):
    sem = refs[-1]
    copies = [pltpu.make_async_copy(refs[n], refs[4 + n], sem.at[n]) for n in range(4)]
    for copy in copies:
        copy.start()
    for copy in copies:
        copy.wait()


def on_device(features, tiles, tile_rows, tile_cols, tile_count, weight, bias, cotangent):
    vmem = pl.BlockSpec(memory_space=pltpu.VMEM)
    hbm = pl.BlockSpec(memory_space=pl.ANY)
    dma = pltpu.SemaphoreType.DMA
    shapes = (
        jax.ShapeDtypeStruct((T, HID), BF16),
        jax.ShapeDtypeStruct((T, T), BF16),
        jax.ShapeDtypeStruct((T, HID), F32),
        jax.ShapeDtypeStruct((1, HID), F32),
    )
    results = pl.pallas_call(
        kernel,
        out_shape=shapes,
        in_specs=[hbm] * 8,
        out_specs=(vmem,) * 4,
        scratch_shapes=[
            pltpu.SMEM((K,), jnp.int32),
            pltpu.SMEM((K,), jnp.int32),
            pltpu.SMEM((1,), jnp.int32),
            pltpu.VMEM((K, T, T), BF16),
            pltpu.VMEM((T, HID), F32),
            pltpu.VMEM((1, HID), F32),
            pltpu.VMEM((T, HID), BF16),
            pltpu.VMEM((NP, T, T), BF16),
            pltpu.VMEM((K + 1, T, T), F32),
            pltpu.VMEM((NZ, T, T), BF16),
            pltpu.VMEM((NZ, T, T), BF16),
            pltpu.VMEM((NZ, T, T), BF16),
            pltpu.VMEM((NZ, T, T), BF16),
            pltpu.VMEM((2 * NZ, T, T), BF16),
            pltpu.VMEM((NP, T, T), BF16),
            pltpu.VMEM((NP, T, T), BF16),
            pltpu.VMEM((NP, 2, 16, T), F32),
            pltpu.VMEM((2 * NP, 16, T), F32),
            pltpu.VMEM((NZ, 16, T), BF16),
            pltpu.VMEM((NP, 2, 16, T), F32),
            dma((8,)),
        ]
        + [dma((16,))] * 12
        + [dma((32,)), dma((32,)), dma((16,)), dma((16,)), dma((32,)), dma((32,))],
        compiler_params=pltpu.CompilerParams(
            collective_id=0, has_side_effects=True, vmem_limit_bytes=60 * 1024 * 1024
        ),
    )(
        features,
        tiles.reshape(K, T, T),
        tile_rows.reshape(K),
        tile_cols.reshape(K),
        tile_count.reshape(1),
        weight,
        bias.reshape(1, HID),
        cotangent,
    )
    out, gf, gw, gb = pl.pallas_call(
        write_out,
        out_shape=shapes,
        in_specs=[vmem] * 4,
        out_specs=(hbm,) * 4,
        scratch_shapes=[dma((4,))],
    )(*results)
    return out, gf, gw, gb.reshape(HID)


def solution(mesh):
    placed = (
        P(("col", "row"), None),
        P("row", "col", None, None, None),
        P("row", "col", None),
        P("row", "col", None),
        P("row", "col"),
        P(),
        P(),
        P(("row", "col"), None),
    )
    return jax.shard_map(
        on_device,
        mesh=mesh,
        in_specs=placed,
        out_specs=(P(("row", "col"), None), P(("col", "row"), None), P(), P()),
        check_vma=False,
    )
```

```python
import jax
import jax.numpy as jnp
from jax import lax
from jax.experimental import pallas as pl
from jax.experimental.pallas import tpu as pltpu
from jax.sharding import PartitionSpec as P

MESH = pl.DeviceIdType.MESH
F32 = jnp.float32
BF16 = jnp.bfloat16
T = 128
K = 16
NX = 4
NY = 4
NZ = 16
NP = NX * NY
BR = 32
NODES = 65536
HID = 256
LEAF = {5: 6, 7: 6, 8: 6, -4: -5, -6: -5, -7: -5, 2: 3, 4: 3, -3: -2}
RELAY = [6, -5, 3, -2]
NEAR = [1, -1]
ORDER = list(LEAF) + NEAR + RELAY + [0]
FAR_FIRST = sorted(range(1, NP), key=lambda i: -min(i // 4, 4 - i // 4) - min(i % 4, 4 - i % 4))
AT = {p: n for n, p in enumerate(ORDER)}
C0 = 0.7978845608028654
C1 = 0.044715


def dot(a, b, dims=((1,), (0,))):
    return lax.dot_general(a, b, (dims, ((), ())), preferred_element_type=F32)


def split(v):
    hi = v.astype(BF16)
    return hi, (v - hi.astype(F32)).astype(BF16)


def kernel(
    feat, tiles_hbm, rows_hbm, cols_hbm, count_hbm, w_hbm, bias_hbm, cot_hbm,
    out, gf, gw, gb,
    rows, cols, count, tiles, w, bias, cot, feats, sums, part, sib, bsend, brecv, dagg, qpart, qrecv,
    epart, erecv, zall, fin,
    in_sem, a_ss, a_rs, p_ss, p_rs, b_ss, b_rs,
    c_ss, c_rs, cs_ss, cs_rs, q_ss, q_rs,
    e_ss, e_rs, z_ss, z_rs, g_ss, g_rs,
):
    r = lax.axis_index("row")
    c = lax.axis_index("col")
    y, x = r // NX, r % NX
    z, core = c // 2, c % 2

    def plane(i):
        return ((y + i // NX) % NY) * NX + (x + i % NX) % NX

    def ring(i):
        return ((z + i) % NZ) * 2 + core

    me_other = (r, z * 2 + 1 - core)
    operands = (
        (feat, feats.at[r]), (rows_hbm, rows), (cols_hbm, cols), (count_hbm, count),
        (tiles_hbm, tiles), (w_hbm, w), (bias_hbm, bias), (cot_hbm, cot),
    )
    loads = [pltpu.make_async_copy(a, b, in_sem.at[n]) for n, (a, b) in enumerate(operands)]
    for copy in loads:
        copy.start()
    def send(src, dst, ssem, rsem, where):
        copy = pltpu.make_async_remote_copy(
            src_ref=src, dst_ref=dst, send_sem=ssem, recv_sem=rsem,
            device_id=where, device_id_type=MESH,
        )
        copy.start()
        return copy

    def wait(ref, sem):
        pltpu.make_async_copy(ref, ref, sem.at[0]).wait()

    barrier = pltpu.get_barrier_semaphore()
    for i in range(1, NP):
        pl.semaphore_signal(barrier, inc=1, device_id=(plane(i), c), device_id_type=MESH)
    for i in range(1, NZ):
        pl.semaphore_signal(barrier, inc=1, device_id=(r, ring(i)), device_id_type=MESH)
    pl.semaphore_signal(barrier, inc=1, device_id=me_other, device_id_type=MESH)
    pl.semaphore_wait(barrier, NP + NZ - 1)

    for i in FAR_FIRST:
        send(feat, feats.at[r], a_ss.at[0], a_rs.at[0], (plane(i), c))

    for copy in loads[1:4]:
        copy.wait()
    live = count[0]
    dead = [NODES * jnp.minimum(jnp.maximum(k + 1 - live, 0), 1) for k in range(K)]
    slot_r = [rows[k] + dead[k] for k in range(K)]
    slot_c = [cols[k] + dead[k] for k in range(K)]

    def latest(slots, n, b):
        found = jnp.int32(0)
        for k in range(n):
            apart = slots[k] - b
            differs = jnp.minimum(jnp.maximum(apart, -apart), 1)
            found = jnp.maximum(found, (k + 1) * (1 - differs))
        return found

    prev_r = [latest(slot_r, k, slot_r[k]) for k in range(K)]
    prev_c = [latest(slot_c, k, slot_c[k]) for k in range(K)]
    last_r = [
        [latest(slot_r, K, ring(NZ - p) // 2 * 2 + half) for p in ORDER]
        for half in (1 - core, core)
    ]
    last_c = [latest(slot_c, K, plane(i)) for i in range(NP)]

    sums[0] = jnp.zeros((T, T), F32)
    for copy in (loads[0], *loads[4:]):
        copy.wait()
    wait(feats.at[pl.ds(0, NP - 1)], a_rs)

    for k in range(K):
        sums[k + 1] = dot(tiles[k], feats[jnp.minimum(jnp.maximum(cols[k], 0), NP - 1)])
    for k in range(1, K):
        sums[k + 1] = sums[k + 1] + sums[prev_r[k]]

    p_copies = []
    for g in range(4):
        for j in range(4 * g, 4 * g + 4):
            part[j] = sums[last_r[0][j]].astype(BF16)
        four = pl.ds(4 * g, 4)
        p_copies.append(
            send(part.at[four], sib.at[four], p_ss.at[0], p_rs.at[g], me_other)
        )

    b_copies = {}

    def own(p):
        j = AT[p]
        if j % 4 == 0:
            p_copies[j // 4].wait_recv()
        return sums[last_r[1][j]] + sib[j].astype(F32)

    def pass_on(p, to):
        v = own(p)
        leaves = [AT[leaf] for leaf, relay in LEAF.items() if relay == p]
        if leaves:
            held = brecv.at[pl.ds(leaves[0], len(leaves))]
            pltpu.make_async_copy(held, held, b_rs.at[RELAY.index(p)]).wait()
        for n in leaves:
            v = v + brecv[n].astype(F32)
        n = AT[p]
        bsend[n] = v.astype(BF16)
        b_copies[p] = send(
            bsend.at[n], brecv.at[n], b_ss.at[0],
            b_rs.at[RELAY.index(to) if to else n - len(LEAF) + 4], (r, ring(NZ + to - p)),
        )

    for p in ORDER[:-1]:
        pass_on(p, LEAF.get(p, 0))
    total = own(0)
    for p in NEAR + RELAY:
        b_copies[p].wait_recv()
        total = total + brecv[AT[p]].astype(F32)
    agg = total.astype(BF16)

    w_hi, w_lo = split(w[...])
    pre = dot(agg, w_hi) + dot(agg, w_lo) + bias[...]
    square = pre * pre
    t = jnp.tanh(C0 * (pre + C1 * (square * pre)))
    half = 0.5 * (1.0 + t)
    slope = half + 0.5 * pre * (1.0 - t * t) * (C0 * (1.0 + 3.0 * C1 * square))
    dpre = cot[...].astype(F32) * slope
    dp_hi, dp_lo = split(dpre)
    back = ((1,), (1,))
    da = dot(dp_hi, w_hi, back) + dot(dp_lo, w_hi, back) + dot(dp_hi, w_lo, back)
    dagg[c] = da.astype(BF16)

    c_copies = {}

    def c_send(p, via):
        block = dagg.at[ring(NZ - via)]
        n = AT[p]
        c_copies[p] = send(
            block, block, c_ss.at[0], c_rs.at[n], (r, ring(NZ + p - via))
        )

    def c_share(p):
        block = dagg.at[ring(NZ - p)]
        send(block, block, cs_ss.at[0], cs_rs.at[0], me_other)

    for p in RELAY + NEAR:
        c_send(p, 0)
    c_share(0)

    out[...] = (pre * half).astype(BF16)
    down0 = ((0,), (0,))
    local_w = dot(agg, dp_hi, down0) + dot(agg, dp_lo, down0)
    local_b = jnp.sum(dpre.reshape(T // 8, 8, HID), axis=0)
    for h in range(2):
        lanes = slice(T * h, T * h + T)
        for p in range(NP):
            piece = (local_w[8 * p : 8 * p + 8, lanes], local_b[:, lanes])
            epart[p, h] = jnp.concatenate(piece, axis=0).astype(BF16)

    cores = (core, 1 - core)
    pairs = [(i, t) for i in FAR_FIRST + [0] for t in (0, 1) if i or t]
    for i, t in pairs:
        send(
            epart.at[plane(i), cores[t]], erecv.at[2 * i + t], e_ss.at[0], e_rs.at[0],
            (plane(i), z * 2 + cores[t]),
        )

    for via in RELAY:
        c_copies[via].wait_recv()
        for p, relay in LEAF.items():
            if relay == via:
                c_send(p, via)
        c_share(via)
    for p in NEAR:
        c_copies[p].wait_recv()
        c_share(p)

    wait(erecv.at[pl.ds(1, 2 * NP - 1)], e_rs)
    acc = epart[r, core].astype(F32)
    for n in range(1, 2 * NP):
        acc = acc + erecv[n].astype(F32)
    zall[z] = acc.astype(BF16)
    for i in (8, 7, 9, 6, 10, 5, 11, 4, 12, 3, 13, 2, 14, 1, 15):
        send(zall.at[z], zall.at[z], z_ss.at[0], z_rs.at[0], (r, ring(i)))

    for p in LEAF:
        c_copies[p].wait_recv()
        c_share(p)
    wait(dagg.at[pl.ds(0, NZ)], cs_rs)

    for k in range(K):
        picked = dagg[jnp.minimum(jnp.maximum(rows[k], 0), BR - 1)]
        sums[k + 1] = dot(tiles[k], picked, down0)
    for k in range(1, K):
        sums[k + 1] = sums[k + 1] + sums[prev_c[k]]
    q_copies = {}
    for i in FAR_FIRST + [0]:
        qpart[i] = sums[last_c[i]].astype(BF16)
        if i:
            q_copies[i] = send(
                qpart.at[i], qrecv.at[i], q_ss.at[0], q_rs.at[i], (plane(i), c)
            )
    wait(feats.at[pl.ds(0, NP - 1)], a_ss)
    wait(part, p_ss)
    wait(bsend.at[pl.ds(0, NZ - 1)], b_ss)
    wait(dagg.at[pl.ds(0, NZ - 1)], c_ss)
    wait(dagg.at[pl.ds(0, NZ)], cs_ss)
    wait(erecv.at[pl.ds(1, 2 * NP - 1)], e_ss)

    wait(zall.at[pl.ds(0, NZ - 1)], z_rs)
    acc = zall[0].astype(F32)
    for i in range(1, NZ):
        acc = acc + zall[i].astype(F32)
    fin[r, core] = acc
    for i, t in pairs:
        piece = fin.at[r, core, pl.ds(0, 8)] if i else fin.at[r, core]
        send(piece, piece, g_ss.at[0], g_rs.at[0], (plane(i), z * 2 + cores[t]))
    wait(zall.at[pl.ds(0, NZ - 1)], z_ss)

    acc = qpart[0].astype(F32)
    for i in FAR_FIRST:
        q_copies[i].wait_recv()
        acc = acc + qrecv[i].astype(F32)
    gf[...] = acc.astype(BF16)
    wait(fin.at[pl.ds(0, NP // 2)], g_rs)
    for h in range(2):
        lanes = slice(T * h, T * h + T)
        for p in range(NP):
            gw[8 * p : 8 * p + 8, lanes] = fin[p, h, 0:8]
        gb[:, lanes] = jnp.sum(fin[r, h, 8:16], axis=0, keepdims=True)
    wait(qrecv.at[pl.ds(0, NP - 1)], q_ss)
    wait(fin.at[pl.ds(0, NP // 2)], g_ss)


def write_out(*refs):
    sem = refs[-1]
    copies = [pltpu.make_async_copy(refs[n], refs[4 + n], sem.at[n]) for n in range(4)]
    for copy in copies:
        copy.start()
    for copy in copies:
        copy.wait()


def on_device(features, tiles, tile_rows, tile_cols, tile_count, weight, bias, cotangent):
    vmem = pl.BlockSpec(memory_space=pltpu.VMEM)
    hbm = pl.BlockSpec(memory_space=pl.ANY)
    dma = pltpu.SemaphoreType.DMA
    shapes = (
        jax.ShapeDtypeStruct((T, HID), BF16),
        jax.ShapeDtypeStruct((T, T), BF16),
        jax.ShapeDtypeStruct((T, HID), F32),
        jax.ShapeDtypeStruct((1, HID), F32),
    )
    results = pl.pallas_call(
        kernel,
        out_shape=shapes,
        in_specs=[hbm] * 8,
        out_specs=(vmem,) * 4,
        scratch_shapes=[
            pltpu.SMEM((K,), jnp.int32),
            pltpu.SMEM((K,), jnp.int32),
            pltpu.SMEM((1,), jnp.int32),
            pltpu.VMEM((K, T, T), BF16),
            pltpu.VMEM((T, HID), F32),
            pltpu.VMEM((1, HID), F32),
            pltpu.VMEM((T, HID), BF16),
            pltpu.VMEM((NP, T, T), BF16),
            pltpu.VMEM((K + 1, T, T), F32),
            pltpu.VMEM((NZ, T, T), BF16),
            pltpu.VMEM((NZ, T, T), BF16),
            pltpu.VMEM((NZ, T, T), BF16),
            pltpu.VMEM((NZ, T, T), BF16),
            pltpu.VMEM((2 * NZ, T, T), BF16),
            pltpu.VMEM((NP, T, T), BF16),
            pltpu.VMEM((NP, T, T), BF16),
            pltpu.VMEM((NP, 2, 16, T), BF16),
            pltpu.VMEM((2 * NP, 16, T), BF16),
            pltpu.VMEM((NZ, 16, T), BF16),
            pltpu.VMEM((NP, 2, 16, T), F32),
        ]
        + [dma((n,)) for n in (8, 1, 1, 1, 4, 1, 10, 1, 15, 1, 1, 1, 16, 1, 1, 1, 1, 1, 1)],
        compiler_params=pltpu.CompilerParams(
            collective_id=0, has_side_effects=True, vmem_limit_bytes=60 * 1024 * 1024
        ),
    )(
        features,
        tiles.reshape(K, T, T),
        tile_rows.reshape(K),
        tile_cols.reshape(K),
        tile_count.reshape(1),
        weight,
        bias.reshape(1, HID),
        cotangent,
    )
    out, gf, gw, gb = pl.pallas_call(
        write_out,
        out_shape=shapes,
        in_specs=[vmem] * 4,
        out_specs=(hbm,) * 4,
        scratch_shapes=[dma((4,))],
    )(*results)
    return out, gf, gw, gb.reshape(HID)


def solution(mesh):
    placed = (
        P(("col", "row"), None),
        P("row", "col", None, None, None),
        P("row", "col", None),
        P("row", "col", None),
        P("row", "col"),
        P(),
        P(),
        P(("row", "col"), None),
    )
    return jax.shard_map(
        on_device,
        mesh=mesh,
        in_specs=placed,
        out_specs=(P(("row", "col"), None), P(("col", "row"), None), P(), P()),
        check_vma=False,
    )
```

```python
import jax
import jax.numpy as jnp
from jax import lax
from jax.experimental import pallas as pl
from jax.experimental.pallas import tpu as pltpu
from jax.sharding import PartitionSpec as P

MESH = pl.DeviceIdType.MESH
F32 = jnp.float32
BF16 = jnp.bfloat16
T = 128
K = 16
NX = 4
NY = 4
NZ = 16
NP = NX * NY
BR = 32
NODES = 65536
HID = 256
LEAF = {8: 5, 7: 5, 6: 5, 4: 5, -7: -5, -6: -5, -4: -5, 3: 2, -3: -2}
RELAY = [5, -5, 2, -2]
NEAR = [1, -1]
ORDER = list(LEAF) + NEAR + RELAY + [0]
FAR_FIRST = sorted(range(1, NP), key=lambda i: -min(i // 4, 4 - i // 4) - min(i % 4, 4 - i % 4))
AT = {p: n for n, p in enumerate(ORDER)}
C0 = 0.7978845608028654
C1 = 0.044715


def dot(a, b, dims=((1,), (0,))):
    return lax.dot_general(a, b, (dims, ((), ())), preferred_element_type=F32)


def split(v):
    hi = v.astype(BF16)
    return hi, (v - hi.astype(F32)).astype(BF16)


def kernel(
    feat, tiles_hbm, rows_hbm, cols_hbm, count_hbm, w_hbm, bias_hbm, cot_hbm,
    out, gf, gw, gb,
    rows, cols, count, tiles, w, bias, cot, feats, sums, part, sib, bsend, brecv, dagg, qpart, qrecv,
    epart, erecv, zall, fin,
    in_sem, a_ss, a_rs, p_ss, p_rs, b_ss, b_rs,
    c_ss, c_rs, cs_ss, cs_rs, q_ss, q_rs,
    e_ss, e_rs, z_ss, z_rs, g_ss, g_rs,
):
    r = lax.axis_index("row")
    c = lax.axis_index("col")
    y, x = r // NX, r % NX
    z, core = c // 2, c % 2

    def plane(i):
        return ((y + i // NX) % NY) * NX + (x + i % NX) % NX

    def ring(i):
        return ((z + i) % NZ) * 2 + core

    me_other = (r, z * 2 + 1 - core)
    operands = (
        (feat, feats.at[r]), (rows_hbm, rows), (cols_hbm, cols), (count_hbm, count),
        (tiles_hbm, tiles), (w_hbm, w), (bias_hbm, bias), (cot_hbm, cot),
    )
    loads = [pltpu.make_async_copy(a, b, in_sem.at[n]) for n, (a, b) in enumerate(operands)]
    for copy in loads:
        copy.start()
    def send(src, dst, ssem, rsem, where):
        copy = pltpu.make_async_remote_copy(
            src_ref=src, dst_ref=dst, send_sem=ssem, recv_sem=rsem,
            device_id=where, device_id_type=MESH,
        )
        copy.start()
        return copy

    def wait(ref, sem):
        pltpu.make_async_copy(ref, ref, sem.at[0]).wait()

    barrier = pltpu.get_barrier_semaphore()
    for i in range(1, NP):
        pl.semaphore_signal(barrier, inc=1, device_id=(plane(i), c), device_id_type=MESH)
    for i in range(1, NZ):
        pl.semaphore_signal(barrier, inc=1, device_id=(r, ring(i)), device_id_type=MESH)
    pl.semaphore_signal(barrier, inc=1, device_id=me_other, device_id_type=MESH)
    pl.semaphore_wait(barrier, NP + NZ - 1)

    for i in FAR_FIRST:
        send(feat, feats.at[r], a_ss.at[0], a_rs.at[0], (plane(i), c))

    for copy in loads[1:4]:
        copy.wait()
    live = count[0]
    dead = [NODES * jnp.minimum(jnp.maximum(k + 1 - live, 0), 1) for k in range(K)]
    slot_r = [rows[k] + dead[k] for k in range(K)]
    slot_c = [cols[k] + dead[k] for k in range(K)]

    def latest(slots, n, b):
        found = jnp.int32(0)
        for k in range(n):
            apart = slots[k] - b
            differs = jnp.minimum(jnp.maximum(apart, -apart), 1)
            found = jnp.maximum(found, (k + 1) * (1 - differs))
        return found

    prev_r = [latest(slot_r, k, slot_r[k]) for k in range(K)]
    prev_c = [latest(slot_c, k, slot_c[k]) for k in range(K)]
    last_r = [
        [latest(slot_r, K, ring(NZ - p) // 2 * 2 + half) for p in ORDER]
        for half in (1 - core, core)
    ]
    last_c = [latest(slot_c, K, plane(i)) for i in range(NP)]

    sums[0] = jnp.zeros((T, T), F32)
    for copy in (loads[0], *loads[4:]):
        copy.wait()
    wait(feats.at[pl.ds(0, NP - 1)], a_rs)

    for k in range(K):
        sums[k + 1] = dot(tiles[k], feats[jnp.minimum(jnp.maximum(cols[k], 0), NP - 1)])
    for k in range(1, K):
        sums[k + 1] = sums[k + 1] + sums[prev_r[k]]

    p_copies = []
    for g in range(4):
        for j in range(4 * g, 4 * g + 4):
            part[j] = sums[last_r[0][j]].astype(BF16)
        four = pl.ds(4 * g, 4)
        p_copies.append(
            send(part.at[four], sib.at[four], p_ss.at[0], p_rs.at[g], me_other)
        )

    b_copies = {}

    def own(p):
        j = AT[p]
        if j % 4 == 0:
            p_copies[j // 4].wait_recv()
        return sums[last_r[1][j]] + sib[j].astype(F32)

    def pass_on(p, to):
        v = own(p)
        leaves = [AT[leaf] for leaf, relay in LEAF.items() if relay == p]
        if leaves:
            held = brecv.at[pl.ds(leaves[0], len(leaves))]
            pltpu.make_async_copy(held, held, b_rs.at[RELAY.index(p)]).wait()
        for n in leaves:
            v = v + brecv[n].astype(F32)
        n = AT[p]
        bsend[n] = v.astype(BF16)
        b_copies[p] = send(
            bsend.at[n], brecv.at[n], b_ss.at[0],
            b_rs.at[RELAY.index(to) if to else n - len(LEAF) + 4], (r, ring(NZ + to - p)),
        )

    for p in ORDER[:-1]:
        pass_on(p, LEAF.get(p, 0))
    total = own(0)
    for p in NEAR + RELAY:
        b_copies[p].wait_recv()
        total = total + brecv[AT[p]].astype(F32)
    agg = total.astype(BF16)

    w_hi, w_lo = split(w[...])
    pre = dot(agg, w_hi) + dot(agg, w_lo) + bias[...]
    square = pre * pre
    t = jnp.tanh(C0 * (pre + C1 * (square * pre)))
    half = 0.5 * (1.0 + t)
    slope = half + 0.5 * pre * (1.0 - t * t) * (C0 * (1.0 + 3.0 * C1 * square))
    dpre = cot[...].astype(F32) * slope
    dp_hi, dp_lo = split(dpre)
    back = ((1,), (1,))
    da = dot(dp_hi, w_hi, back) + dot(dp_lo, w_hi, back) + dot(dp_hi, w_lo, back)
    dagg[c] = da.astype(BF16)

    c_copies = {}

    def c_send(p, via):
        block = dagg.at[ring(NZ - via)]
        n = AT[p]
        c_copies[p] = send(
            block, block, c_ss.at[0], c_rs.at[n], (r, ring(NZ + p - via))
        )

    def c_share(p):
        block = dagg.at[ring(NZ - p)]
        send(block, block, cs_ss.at[0], cs_rs.at[0], me_other)

    for p in RELAY + NEAR:
        c_send(p, 0)
    c_share(0)

    out[...] = (pre * half).astype(BF16)
    down0 = ((0,), (0,))
    local_w = dot(agg, dp_hi, down0) + dot(agg, dp_lo, down0)
    local_b = jnp.sum(dpre.reshape(T // 8, 8, HID), axis=0)
    for h in range(2):
        lanes = slice(T * h, T * h + T)
        for p in range(NP):
            piece = (local_w[8 * p : 8 * p + 8, lanes], local_b[:, lanes])
            epart[p, h] = jnp.concatenate(piece, axis=0).astype(BF16)

    cores = (core, 1 - core)
    pairs = [(i, t) for i in FAR_FIRST + [0] for t in (0, 1) if i or t]
    for i, t in pairs:
        send(
            epart.at[plane(i), cores[t]], erecv.at[2 * i + t], e_ss.at[0], e_rs.at[0],
            (plane(i), z * 2 + cores[t]),
        )

    for via in RELAY:
        c_copies[via].wait_recv()
        for p, relay in LEAF.items():
            if relay == via:
                c_send(p, via)
        c_share(via)
    for p in NEAR:
        c_copies[p].wait_recv()
        c_share(p)

    for turn, p in enumerate(LEAF):
        c_copies[p].wait_recv()
        c_share(p)
        if turn == 3:
            wait(erecv.at[pl.ds(1, 2 * NP - 1)], e_rs)
            acc = epart[r, core].astype(F32)
            for n in range(1, 2 * NP):
                acc = acc + erecv[n].astype(F32)
            zall[z] = acc.astype(BF16)
            for i in (8, 7, 9, 6, 10, 5, 11, 4, 12, 3, 13, 2, 14, 1, 15):
                send(zall.at[z], zall.at[z], z_ss.at[0], z_rs.at[0], (r, ring(i)))

    wait(dagg.at[pl.ds(0, NZ)], cs_rs)

    for k in range(K):
        picked = dagg[jnp.minimum(jnp.maximum(rows[k], 0), BR - 1)]
        sums[k + 1] = dot(tiles[k], picked, down0)
    for k in range(1, K):
        sums[k + 1] = sums[k + 1] + sums[prev_c[k]]
    q_copies = {}
    for i in FAR_FIRST + [0]:
        qpart[i] = sums[last_c[i]].astype(BF16)
        if i:
            q_copies[i] = send(
                qpart.at[i], qrecv.at[i], q_ss.at[0], q_rs.at[i], (plane(i), c)
            )
    wait(feats.at[pl.ds(0, NP - 1)], a_ss)
    wait(part, p_ss)
    wait(bsend.at[pl.ds(0, NZ - 1)], b_ss)
    wait(dagg.at[pl.ds(0, NZ - 1)], c_ss)
    wait(dagg.at[pl.ds(0, NZ)], cs_ss)
    wait(erecv.at[pl.ds(1, 2 * NP - 1)], e_ss)

    wait(zall.at[pl.ds(0, NZ - 1)], z_rs)
    acc = zall[0].astype(F32)
    for i in range(1, NZ):
        acc = acc + zall[i].astype(F32)
    fin[r, core] = acc
    for i, t in pairs:
        piece = fin.at[r, core, pl.ds(0, 8)] if i else fin.at[r, core]
        send(piece, piece, g_ss.at[0], g_rs.at[0], (plane(i), z * 2 + cores[t]))
    wait(zall.at[pl.ds(0, NZ - 1)], z_ss)

    acc = qpart[0].astype(F32)
    for i in FAR_FIRST:
        q_copies[i].wait_recv()
        acc = acc + qrecv[i].astype(F32)
    gf[...] = acc.astype(BF16)
    wait(fin.at[pl.ds(0, NP // 2)], g_rs)
    for h in range(2):
        lanes = slice(T * h, T * h + T)
        for p in range(NP):
            gw[8 * p : 8 * p + 8, lanes] = fin[p, h, 0:8]
        gb[:, lanes] = jnp.sum(fin[r, h, 8:16], axis=0, keepdims=True)
    wait(qrecv.at[pl.ds(0, NP - 1)], q_ss)
    wait(fin.at[pl.ds(0, NP // 2)], g_ss)


def write_out(*refs):
    sem = refs[-1]
    copies = [pltpu.make_async_copy(refs[n], refs[4 + n], sem.at[n]) for n in range(4)]
    for copy in copies:
        copy.start()
    for copy in copies:
        copy.wait()


def on_device(features, tiles, tile_rows, tile_cols, tile_count, weight, bias, cotangent):
    vmem = pl.BlockSpec(memory_space=pltpu.VMEM)
    hbm = pl.BlockSpec(memory_space=pl.ANY)
    dma = pltpu.SemaphoreType.DMA
    shapes = (
        jax.ShapeDtypeStruct((T, HID), BF16),
        jax.ShapeDtypeStruct((T, T), BF16),
        jax.ShapeDtypeStruct((T, HID), F32),
        jax.ShapeDtypeStruct((1, HID), F32),
    )
    results = pl.pallas_call(
        kernel,
        out_shape=shapes,
        in_specs=[hbm] * 8,
        out_specs=(vmem,) * 4,
        scratch_shapes=[
            pltpu.SMEM((K,), jnp.int32),
            pltpu.SMEM((K,), jnp.int32),
            pltpu.SMEM((1,), jnp.int32),
            pltpu.VMEM((K, T, T), BF16),
            pltpu.VMEM((T, HID), F32),
            pltpu.VMEM((1, HID), F32),
            pltpu.VMEM((T, HID), BF16),
            pltpu.VMEM((NP, T, T), BF16),
            pltpu.VMEM((K + 1, T, T), F32),
            pltpu.VMEM((NZ, T, T), BF16),
            pltpu.VMEM((NZ, T, T), BF16),
            pltpu.VMEM((NZ, T, T), BF16),
            pltpu.VMEM((NZ, T, T), BF16),
            pltpu.VMEM((2 * NZ, T, T), BF16),
            pltpu.VMEM((NP, T, T), BF16),
            pltpu.VMEM((NP, T, T), BF16),
            pltpu.VMEM((NP, 2, 16, T), BF16),
            pltpu.VMEM((2 * NP, 16, T), BF16),
            pltpu.VMEM((NZ, 16, T), BF16),
            pltpu.VMEM((NP, 2, 16, T), F32),
        ]
        + [dma((n,)) for n in (8, 1, 1, 1, 4, 1, 10, 1, 15, 1, 1, 1, 16, 1, 1, 1, 1, 1, 1)],
        compiler_params=pltpu.CompilerParams(
            collective_id=0, has_side_effects=True, vmem_limit_bytes=60 * 1024 * 1024
        ),
    )(
        features,
        tiles.reshape(K, T, T),
        tile_rows.reshape(K),
        tile_cols.reshape(K),
        tile_count.reshape(1),
        weight,
        bias.reshape(1, HID),
        cotangent,
    )
    out, gf, gw, gb = pl.pallas_call(
        write_out,
        out_shape=shapes,
        in_specs=[vmem] * 4,
        out_specs=(hbm,) * 4,
        scratch_shapes=[dma((4,))],
    )(*results)
    return out, gf, gw, gb.reshape(HID)


def solution(mesh):
    placed = (
        P(("col", "row"), None),
        P("row", "col", None, None, None),
        P("row", "col", None),
        P("row", "col", None),
        P("row", "col"),
        P(),
        P(),
        P(("row", "col"), None),
    )
    return jax.shard_map(
        on_device,
        mesh=mesh,
        in_specs=placed,
        out_specs=(P(("row", "col"), None), P(("col", "row"), None), P(), P()),
        check_vma=False,
    )
```

```python
import jax
import jax.numpy as jnp
from jax import lax
from jax.experimental import pallas as pl
from jax.experimental.pallas import tpu as pltpu
from jax.sharding import PartitionSpec as P

MESH = pl.DeviceIdType.MESH
F32 = jnp.float32
BF16 = jnp.bfloat16
T = 128
K = 16
NX = 4
NY = 4
NZ = 16
NP = NX * NY
BR = 32
NODES = 65536
HID = 256
LEAF = {8: 5, 7: 5, 6: 5, 4: 5, -7: -5, -6: -5, -4: -5, 3: 2, -3: -2}
RELAY = [5, -5, 2, -2]
NEAR = [1, -1]
ORDER = list(LEAF) + NEAR + RELAY + [0]
FAR_FIRST = sorted(range(1, NP), key=lambda i: -min(i // 4, 4 - i // 4) - min(i % 4, 4 - i % 4))
AT = {p: n for n, p in enumerate(ORDER)}
C0 = 0.7978845608028654
C1 = 0.044715


def dot(a, b, dims=((1,), (0,))):
    return lax.dot_general(a, b, (dims, ((), ())), preferred_element_type=F32)


def split(v):
    hi = v.astype(BF16)
    return hi, (v - hi.astype(F32)).astype(BF16)


def kernel(
    feat, tiles_hbm, rows_hbm, cols_hbm, count_hbm, w_hbm, bias_hbm, cot_hbm,
    out, gf, gw, gb,
    rows, cols, count, tiles, w, bias, cot, feats, sums, part, sib, wsplit, bsend, brecv, dagg, qpart, qrecv,
    epart, erecv, zall, fin,
    in_sem, a_ss, a_rs, p_ss, p_rs, b_ss, b_rs,
    c_ss, c_rs, cs_ss, cs_rs, q_ss, q_rs,
    e_ss, e_rs, z_ss, z_rs, g_ss, g_rs,
):
    r = lax.axis_index("row")
    c = lax.axis_index("col")
    y, x = r // NX, r % NX
    z, core = c // 2, c % 2

    def plane(i):
        return ((y + i // NX) % NY) * NX + (x + i % NX) % NX

    def ring(i):
        return ((z + i) % NZ) * 2 + core

    me_other = (r, z * 2 + 1 - core)
    operands = (
        (feat, feats.at[r]), (rows_hbm, rows), (cols_hbm, cols), (count_hbm, count),
        (tiles_hbm, tiles), (w_hbm, w), (bias_hbm, bias), (cot_hbm, cot),
    )
    loads = [pltpu.make_async_copy(a, b, in_sem.at[n]) for n, (a, b) in enumerate(operands)]
    for copy in loads:
        copy.start()
    def send(src, dst, ssem, rsem, where):
        copy = pltpu.make_async_remote_copy(
            src_ref=src, dst_ref=dst, send_sem=ssem, recv_sem=rsem,
            device_id=where, device_id_type=MESH,
        )
        copy.start()
        return copy

    def wait(ref, sem):
        pltpu.make_async_copy(ref, ref, sem.at[0]).wait()

    barrier = pltpu.get_barrier_semaphore()
    for i in range(1, NP):
        pl.semaphore_signal(barrier, inc=1, device_id=(plane(i), c), device_id_type=MESH)
    for i in range(1, NZ):
        pl.semaphore_signal(barrier, inc=1, device_id=(r, ring(i)), device_id_type=MESH)
    pl.semaphore_signal(barrier, inc=1, device_id=me_other, device_id_type=MESH)
    pl.semaphore_wait(barrier, NP + NZ - 1)

    for i in FAR_FIRST:
        send(feat, feats.at[r], a_ss.at[0], a_rs.at[0], (plane(i), c))

    for copy in loads[1:4]:
        copy.wait()
    live = count[0]
    dead = [NODES * jnp.minimum(jnp.maximum(k + 1 - live, 0), 1) for k in range(K)]
    slot_r = [rows[k] + dead[k] for k in range(K)]
    slot_c = [cols[k] + dead[k] for k in range(K)]

    def latest(slots, n, b):
        found = jnp.int32(0)
        for k in range(n):
            apart = slots[k] - b
            differs = jnp.minimum(jnp.maximum(apart, -apart), 1)
            found = jnp.maximum(found, (k + 1) * (1 - differs))
        return found

    prev_r = [latest(slot_r, k, slot_r[k]) for k in range(K)]
    prev_c = [latest(slot_c, k, slot_c[k]) for k in range(K)]
    last_r = [
        [latest(slot_r, K, ring(NZ - p) // 2 * 2 + half) for p in ORDER]
        for half in (1 - core, core)
    ]
    last_c = [latest(slot_c, K, plane(i)) for i in range(NP)]

    sums[0] = jnp.zeros((T, T), F32)
    for copy in (loads[0], *loads[4:]):
        copy.wait()
    wait(feats.at[pl.ds(0, NP - 1)], a_rs)

    for k in range(K):
        sums[k + 1] = dot(tiles[k], feats[jnp.minimum(jnp.maximum(cols[k], 0), NP - 1)])
    for k in range(1, K):
        sums[k + 1] = sums[k + 1] + sums[prev_r[k]]

    p_copies = []
    for g in range(4):
        for j in range(4 * g, 4 * g + 4):
            part[j] = sums[last_r[0][j]].astype(BF16)
        four = pl.ds(4 * g, 4)
        p_copies.append(
            send(part.at[four], sib.at[four], p_ss.at[0], p_rs.at[g], me_other)
        )

    halves = (pl.ds(0, T // 2), pl.ds(T // 2, T // 2))
    signs = (1, -1)
    b_copies = {}
    waited = set()

    def own(h, p):
        j = AT[(signs[h] * p + 7) % NZ - 7]
        if j // 4 not in waited:
            p_copies[j // 4].wait_recv()
            waited.add(j // 4)
        return sums[last_r[1][j], halves[h]] + sib[j, halves[h]].astype(F32)

    def pass_on(h, p, to):
        v = own(h, p)
        leaves = [AT[leaf] for leaf, relay in LEAF.items() if relay == p]
        if leaves:
            held = brecv.at[pl.ds(leaves[0], len(leaves)), halves[h]]
            pltpu.make_async_copy(held, held, b_rs.at[10 * h + RELAY.index(p)]).wait()
        for n in leaves:
            v = v + brecv[n, halves[h]].astype(F32)
        n = AT[p]
        bsend[n, halves[h]] = v.astype(BF16)
        b_copies[h, p] = send(
            bsend.at[n, halves[h]], brecv.at[n, halves[h]], b_ss.at[0],
            b_rs.at[10 * h + (RELAY.index(to) if to else n - len(LEAF) + 4)],
            (r, ring(NZ + signs[h] * (to - p))),
        )

    for h in range(2):
        for p in list(LEAF) + NEAR:
            pass_on(h, p, LEAF.get(p, 0))
    w_hi, w_lo = split(w[...])
    wsplit[0] = w_hi
    wsplit[1] = w_lo
    for h in range(2):
        for p in RELAY:
            pass_on(h, p, 0)

    c_copies = {}

    def c_send(h, p, via):
        block = dagg.at[ring(NZ - signs[h] * via), halves[h]]
        c_copies[h, p] = send(
            block, block, c_ss.at[0], c_rs.at[15 * h + AT[p]], (r, ring(NZ + signs[h] * (p - via)))
        )

    def c_share(h, p):
        block = dagg.at[ring(NZ - signs[h] * p), halves[h]]
        send(block, block, cs_ss.at[0], cs_rs.at[0], me_other)

    back, down0 = ((1,), (1,)), ((0,), (0,))
    local_w = local_b = 0.0
    for h in range(2):
        total = own(h, 0)
        for p in NEAR + RELAY:
            b_copies[h, p].wait_recv()
            total = total + brecv[AT[p], halves[h]].astype(F32)
        agg = total.astype(BF16)
        w_hi, w_lo = wsplit[0], wsplit[1]
        pre = dot(agg, w_hi) + dot(agg, w_lo) + bias[...]
        square = pre * pre
        t = jnp.tanh(C0 * (pre + C1 * (square * pre)))
        half = 0.5 * (1.0 + t)
        slope = half + 0.5 * pre * (1.0 - t * t) * (C0 * (1.0 + 3.0 * C1 * square))
        dpre = cot[halves[h], :].astype(F32) * slope
        dp_hi, dp_lo = split(dpre)
        da = dot(dp_hi, w_hi, back) + dot(dp_lo, w_hi, back) + dot(dp_hi, w_lo, back)
        dagg[c, halves[h]] = da.astype(BF16)
        for p in RELAY + NEAR:
            c_send(h, p, 0)
        c_share(h, 0)
        out[halves[h], :] = (pre * half).astype(BF16)
        local_w = local_w + dot(agg, dp_hi, down0) + dot(agg, dp_lo, down0)
        local_b = local_b + jnp.sum(dpre.reshape(T // 16, 8, HID), axis=0)

    for h in range(2):
        lanes = slice(T * h, T * h + T)
        for p in range(NP):
            piece = (local_w[8 * p : 8 * p + 8, lanes], local_b[:, lanes])
            epart[p, h] = jnp.concatenate(piece, axis=0).astype(BF16)

    cores = (core, 1 - core)
    pairs = [(i, t) for i in FAR_FIRST + [0] for t in (0, 1) if i or t]
    for i, t in pairs:
        send(
            epart.at[plane(i), cores[t]], erecv.at[2 * i + t], e_ss.at[0], e_rs.at[0],
            (plane(i), z * 2 + cores[t]),
        )

    for h in range(2):
        for via in RELAY:
            c_copies[h, via].wait_recv()
            for p, relay in LEAF.items():
                if relay == via:
                    c_send(h, p, via)
            c_share(h, via)
        for p in NEAR:
            c_copies[h, p].wait_recv()
            c_share(h, p)

    for turn, (h, p) in enumerate((h, p) for h in range(2) for p in LEAF):
        c_copies[h, p].wait_recv()
        c_share(h, p)
        if turn == 12:
            wait(erecv.at[pl.ds(1, 2 * NP - 1)], e_rs)
            acc = epart[r, core].astype(F32)
            for n in range(1, 2 * NP):
                acc = acc + erecv[n].astype(F32)
            zall[z] = acc.astype(BF16)
            for i in (8, 7, 9, 6, 10, 5, 11, 4, 12, 3, 13, 2, 14, 1, 15):
                send(zall.at[z], zall.at[z], z_ss.at[0], z_rs.at[0], (r, ring(i)))

    wait(dagg.at[pl.ds(0, NZ)], cs_rs)

    for k in range(K):
        picked = dagg[jnp.minimum(jnp.maximum(rows[k], 0), BR - 1)]
        sums[k + 1] = dot(tiles[k], picked, down0)
    for k in range(1, K):
        sums[k + 1] = sums[k + 1] + sums[prev_c[k]]
    q_copies = {}
    for i in FAR_FIRST + [0]:
        qpart[i] = sums[last_c[i]].astype(BF16)
        if i:
            q_copies[i] = send(
                qpart.at[i], qrecv.at[i], q_ss.at[0], q_rs.at[i], (plane(i), c)
            )
    wait(feats.at[pl.ds(0, NP - 1)], a_ss)
    wait(part, p_ss)
    wait(bsend.at[pl.ds(0, NZ - 1)], b_ss)
    wait(dagg.at[pl.ds(0, NZ - 1)], c_ss)
    wait(dagg.at[pl.ds(0, NZ)], cs_ss)
    wait(erecv.at[pl.ds(1, 2 * NP - 1)], e_ss)

    wait(zall.at[pl.ds(0, NZ - 1)], z_rs)
    acc = zall[0].astype(F32)
    for i in range(1, NZ):
        acc = acc + zall[i].astype(F32)
    fin[r, core] = acc
    for i, t in pairs:
        piece = fin.at[r, core, pl.ds(0, 8)] if i else fin.at[r, core]
        send(piece, piece, g_ss.at[0], g_rs.at[0], (plane(i), z * 2 + cores[t]))
    wait(zall.at[pl.ds(0, NZ - 1)], z_ss)

    acc = qpart[0].astype(F32)
    for i in FAR_FIRST:
        q_copies[i].wait_recv()
        acc = acc + qrecv[i].astype(F32)
    gf[...] = acc.astype(BF16)
    wait(fin.at[pl.ds(0, NP // 2)], g_rs)
    for h in range(2):
        lanes = slice(T * h, T * h + T)
        for p in range(NP):
            gw[8 * p : 8 * p + 8, lanes] = fin[p, h, 0:8]
        gb[:, lanes] = jnp.sum(fin[r, h, 8:16], axis=0, keepdims=True)
    wait(qrecv.at[pl.ds(0, NP - 1)], q_ss)
    wait(fin.at[pl.ds(0, NP // 2)], g_ss)


def write_out(*refs):
    sem = refs[-1]
    copies = [pltpu.make_async_copy(refs[n], refs[4 + n], sem.at[n]) for n in range(4)]
    for copy in copies:
        copy.start()
    for copy in copies:
        copy.wait()


def on_device(features, tiles, tile_rows, tile_cols, tile_count, weight, bias, cotangent):
    vmem = pl.BlockSpec(memory_space=pltpu.VMEM)
    hbm = pl.BlockSpec(memory_space=pl.ANY)
    dma = pltpu.SemaphoreType.DMA
    shapes = (
        jax.ShapeDtypeStruct((T, HID), BF16),
        jax.ShapeDtypeStruct((T, T), BF16),
        jax.ShapeDtypeStruct((T, HID), F32),
        jax.ShapeDtypeStruct((1, HID), F32),
    )
    results = pl.pallas_call(
        kernel,
        out_shape=shapes,
        in_specs=[hbm] * 8,
        out_specs=(vmem,) * 4,
        scratch_shapes=[
            pltpu.SMEM((K,), jnp.int32),
            pltpu.SMEM((K,), jnp.int32),
            pltpu.SMEM((1,), jnp.int32),
            pltpu.VMEM((K, T, T), BF16),
            pltpu.VMEM((T, HID), F32),
            pltpu.VMEM((1, HID), F32),
            pltpu.VMEM((T, HID), BF16),
            pltpu.VMEM((NP, T, T), BF16),
            pltpu.VMEM((K + 1, T, T), F32),
            pltpu.VMEM((NZ, T, T), BF16),
            pltpu.VMEM((NZ, T, T), BF16),
            pltpu.VMEM((2, T, HID), BF16),
            pltpu.VMEM((NZ, T, T), BF16),
            pltpu.VMEM((NZ, T, T), BF16),
            pltpu.VMEM((2 * NZ, T, T), BF16),
            pltpu.VMEM((NP, T, T), BF16),
            pltpu.VMEM((NP, T, T), BF16),
            pltpu.VMEM((NP, 2, 16, T), BF16),
            pltpu.VMEM((2 * NP, 16, T), BF16),
            pltpu.VMEM((NZ, 16, T), BF16),
            pltpu.VMEM((NP, 2, 16, T), F32),
        ]
        + [dma((n,)) for n in (8, 1, 1, 1, 4, 1, 20, 1, 30, 1, 1, 1, 16, 1, 1, 1, 1, 1, 1)],
        compiler_params=pltpu.CompilerParams(
            collective_id=0, has_side_effects=True, vmem_limit_bytes=60 * 1024 * 1024
        ),
    )(
        features,
        tiles.reshape(K, T, T),
        tile_rows.reshape(K),
        tile_cols.reshape(K),
        tile_count.reshape(1),
        weight,
        bias.reshape(1, HID),
        cotangent,
    )
    out, gf, gw, gb = pl.pallas_call(
        write_out,
        out_shape=shapes,
        in_specs=[vmem] * 4,
        out_specs=(hbm,) * 4,
        scratch_shapes=[dma((4,))],
    )(*results)
    return out, gf, gw, gb.reshape(HID)


def solution(mesh):
    placed = (
        P(("col", "row"), None),
        P("row", "col", None, None, None),
        P("row", "col", None),
        P("row", "col", None),
        P("row", "col"),
        P(),
        P(),
        P(("row", "col"), None),
    )
    return jax.shard_map(
        on_device,
        mesh=mesh,
        in_specs=placed,
        out_specs=(P(("row", "col"), None), P(("col", "row"), None), P(), P()),
        check_vma=False,
    )
```

```python
import jax
import jax.numpy as jnp
from jax import lax
from jax.experimental import pallas as pl
from jax.experimental.pallas import tpu as pltpu
from jax.sharding import PartitionSpec as P

MESH = pl.DeviceIdType.MESH
F32 = jnp.float32
BF16 = jnp.bfloat16
T = 128
K = 16
NX = 4
NY = 4
NZ = 16
NP = NX * NY
BR = 32
NODES = 65536
HID = 256
LEAF = {8: 5, 7: 5, 6: 5, 4: 5, -7: -5, -6: -5, -4: -5, 3: 2, -3: -2}
RELAY = [5, -5, 2, -2]
NEAR = [1, -1]
ORDER = list(LEAF) + NEAR + RELAY + [0]
FAR_FIRST = sorted(range(1, NP), key=lambda i: -min(i // 4, 4 - i // 4) - min(i % 4, 4 - i % 4))
AT = {p: n for n, p in enumerate(ORDER)}
ZNEAR = [1, 2, 3, 5, 11, 13, 14, 15]
C0 = 0.7978845608028654
C1 = 0.044715


def dot(a, b, dims=((1,), (0,))):
    return lax.dot_general(a, b, (dims, ((), ())), preferred_element_type=F32)


def split(v):
    hi = v.astype(BF16)
    return hi, (v - hi.astype(F32)).astype(BF16)


def kernel(
    feat, tiles_hbm, rows_hbm, cols_hbm, count_hbm, w_hbm, bias_hbm, cot_hbm,
    out, gf, gw, gb,
    rows, cols, count, tiles, w, bias, cot, feats, sums, part, sib, wsplit, bsend, brecv, dagg, qpart, qrecv,
    epart, erecv, zall, fin,
    in_sem, a_ss, a_rs, p_ss, p_rs, b_ss, b_rs,
    c_ss, c_rs, cs_ss, cs_rs, q_ss, q_rs,
    e_ss, e_rs, z_ss, z_rs, g_ss, g_rs,
):
    r = lax.axis_index("row")
    c = lax.axis_index("col")
    y, x = r // NX, r % NX
    z, core = c // 2, c % 2

    def plane(i):
        return ((y + i // NX) % NY) * NX + (x + i % NX) % NX

    def ring(i):
        return ((z + i) % NZ) * 2 + core

    me_other = (r, z * 2 + 1 - core)
    operands = (
        (feat, feats.at[r]), (rows_hbm, rows), (cols_hbm, cols), (count_hbm, count),
        (tiles_hbm, tiles), (w_hbm, w), (bias_hbm, bias), (cot_hbm, cot),
    )
    loads = [pltpu.make_async_copy(a, b, in_sem.at[n]) for n, (a, b) in enumerate(operands)]
    for copy in loads:
        copy.start()
    def send(src, dst, ssem, rsem, where):
        copy = pltpu.make_async_remote_copy(
            src_ref=src, dst_ref=dst, send_sem=ssem, recv_sem=rsem,
            device_id=where, device_id_type=MESH,
        )
        copy.start()
        return copy

    def wait(ref, sem):
        pltpu.make_async_copy(ref, ref, sem.at[0]).wait()

    barrier = pltpu.get_barrier_semaphore()
    for i in range(1, NP):
        pl.semaphore_signal(barrier, inc=1, device_id=(plane(i), c), device_id_type=MESH)
    for i in ZNEAR:
        pl.semaphore_signal(barrier, inc=1, device_id=(r, ring(i)), device_id_type=MESH)
    pl.semaphore_signal(barrier, inc=1, device_id=me_other, device_id_type=MESH)
    pl.semaphore_wait(barrier, NP + len(ZNEAR))

    for i in FAR_FIRST:
        send(feat, feats.at[r], a_ss.at[0], a_rs.at[0], (plane(i), c))

    for copy in loads[1:4]:
        copy.wait()
    live = count[0]
    dead = [NODES * jnp.minimum(jnp.maximum(k + 1 - live, 0), 1) for k in range(K)]
    slot_r = [rows[k] + dead[k] for k in range(K)]
    slot_c = [cols[k] + dead[k] for k in range(K)]

    def latest(slots, n, b):
        found = jnp.int32(0)
        for k in range(n):
            apart = slots[k] - b
            differs = jnp.minimum(jnp.maximum(apart, -apart), 1)
            found = jnp.maximum(found, (k + 1) * (1 - differs))
        return found

    prev_r = [latest(slot_r, k, slot_r[k]) for k in range(K)]
    prev_c = [latest(slot_c, k, slot_c[k]) for k in range(K)]
    last_r = [
        [latest(slot_r, K, ring(NZ - p) // 2 * 2 + half) for p in ORDER]
        for half in (1 - core, core)
    ]
    last_c = [latest(slot_c, K, plane(i)) for i in range(NP)]

    sums[0] = jnp.zeros((T, T), F32)
    for copy in (loads[0], *loads[4:]):
        copy.wait()
    wait(feats.at[pl.ds(0, NP - 1)], a_rs)

    for k in range(K):
        sums[k + 1] = dot(tiles[k], feats[jnp.minimum(jnp.maximum(cols[k], 0), NP - 1)])
    for k in range(1, K):
        sums[k + 1] = sums[k + 1] + sums[prev_r[k]]

    p_copies = []
    for g in range(4):
        for j in range(4 * g, 4 * g + 4):
            part[j] = sums[last_r[0][j]].astype(BF16)
        four = pl.ds(4 * g, 4)
        p_copies.append(
            send(part.at[four], sib.at[four], p_ss.at[0], p_rs.at[g], me_other)
        )

    halves = (pl.ds(0, T // 2), pl.ds(T // 2, T // 2))
    signs = (1, -1)
    b_copies = {}
    waited = set()

    def own(h, p):
        j = AT[(signs[h] * p + 7) % NZ - 7]
        if j // 4 not in waited:
            p_copies[j // 4].wait_recv()
            waited.add(j // 4)
        return sums[last_r[1][j], halves[h]] + sib[j, halves[h]].astype(F32)

    def pass_on(h, p, to):
        v = own(h, p)
        leaves = [AT[leaf] for leaf, relay in LEAF.items() if relay == p]
        if leaves:
            held = brecv.at[pl.ds(leaves[0], len(leaves)), halves[h]]
            pltpu.make_async_copy(held, held, b_rs.at[10 * h + RELAY.index(p)]).wait()
        for n in leaves:
            v = v + brecv[n, halves[h]].astype(F32)
        n = AT[p]
        bsend[n, halves[h]] = v.astype(BF16)
        b_copies[h, p] = send(
            bsend.at[n, halves[h]], brecv.at[n, halves[h]], b_ss.at[0],
            b_rs.at[10 * h + (RELAY.index(to) if to else n - len(LEAF) + 4)],
            (r, ring(NZ + signs[h] * (to - p))),
        )

    for h in range(2):
        for p in list(LEAF) + NEAR:
            pass_on(h, p, LEAF.get(p, 0))
    w_hi, w_lo = split(w[...])
    wsplit[0] = w_hi
    wsplit[1] = w_lo
    for h in range(2):
        for p in RELAY:
            pass_on(h, p, 0)

    c_copies = {}

    def c_send(h, p, via):
        block = dagg.at[ring(NZ - signs[h] * via), halves[h]]
        c_copies[h, p] = send(
            block, block, c_ss.at[0], c_rs.at[15 * h + AT[p]], (r, ring(NZ + signs[h] * (p - via)))
        )

    def c_share(h, p):
        block = dagg.at[ring(NZ - signs[h] * p), halves[h]]
        send(block, block, cs_ss.at[0], cs_rs.at[0], me_other)

    back, down0 = ((1,), (1,)), ((0,), (0,))
    kept = []
    for h in range(2):
        total = own(h, 0)
        for p in NEAR + RELAY:
            b_copies[h, p].wait_recv()
            total = total + brecv[AT[p], halves[h]].astype(F32)
        agg = total.astype(BF16)
        w_hi, w_lo = wsplit[0], wsplit[1]
        pre = dot(agg, w_hi) + dot(agg, w_lo) + bias[...]
        square = pre * pre
        t = jnp.tanh(C0 * (pre + C1 * (square * pre)))
        half = 0.5 * (1.0 + t)
        slope = half + 0.5 * pre * (1.0 - t * t) * (C0 * (1.0 + 3.0 * C1 * square))
        dpre = cot[halves[h], :].astype(F32) * slope
        dp_hi, dp_lo = split(dpre)
        da = dot(dp_hi, w_hi, back) + dot(dp_lo, w_hi, back) + dot(dp_hi, w_lo, back)
        dagg[c, halves[h]] = da.astype(BF16)
        for p in RELAY + NEAR:
            c_send(h, p, 0)
        c_share(h, 0)
        out[halves[h], :] = (pre * half).astype(BF16)
        kept.append((agg, dp_hi, dp_lo, dpre))

    local_w = local_b = 0.0
    for agg, dp_hi, dp_lo, dpre in kept:
        local_w = local_w + dot(agg, dp_hi, down0) + dot(agg, dp_lo, down0)
        local_b = local_b + jnp.sum(dpre.reshape(T // 16, 8, HID), axis=0)
    for h in range(2):
        lanes = slice(T * h, T * h + T)
        for p in range(NP):
            piece = (local_w[8 * p : 8 * p + 8, lanes], local_b[:, lanes])
            epart[p, h] = jnp.concatenate(piece, axis=0).astype(BF16)

    cores = (core, 1 - core)
    pairs = [(i, t) for i in FAR_FIRST + [0] for t in (0, 1) if i or t]
    for i, t in pairs:
        send(
            epart.at[plane(i), cores[t]], erecv.at[2 * i + t], e_ss.at[0], e_rs.at[0],
            (plane(i), z * 2 + cores[t]),
        )

    for h in range(2):
        for via in RELAY:
            c_copies[h, via].wait_recv()
            for p, relay in LEAF.items():
                if relay == via:
                    c_send(h, p, via)
            c_share(h, via)
        for p in NEAR:
            c_copies[h, p].wait_recv()
            c_share(h, p)

    z_copies = {}

    def z_send(p, via):
        slot = zall.at[(z + NZ - via) % NZ]
        z_copies[p] = send(
            slot, slot, z_ss.at[0], z_rs.at[AT[p]], (r, ring(NZ + p - via))
        )

    for turn, (h, p) in enumerate((h, p) for h in range(2) for p in LEAF):
        c_copies[h, p].wait_recv()
        c_share(h, p)
        if turn == 8:
            wait(erecv.at[pl.ds(1, 2 * NP - 1)], e_rs)
            acc = epart[r, core].astype(F32)
            for n in range(1, 2 * NP):
                acc = acc + erecv[n].astype(F32)
            zall[z] = acc.astype(BF16)
            for p in RELAY + NEAR:
                z_send(p, 0)

    wait(dagg.at[pl.ds(0, NZ)], cs_rs)

    for k in range(K):
        picked = dagg[jnp.minimum(jnp.maximum(rows[k], 0), BR - 1)]
        sums[k + 1] = dot(tiles[k], picked, down0)
    for k in range(1, K):
        sums[k + 1] = sums[k + 1] + sums[prev_c[k]]
    q_copies = {}
    for i in FAR_FIRST + [0]:
        qpart[i] = sums[last_c[i]].astype(BF16)
        if i:
            q_copies[i] = send(
                qpart.at[i], qrecv.at[i], q_ss.at[0], q_rs.at[i], (plane(i), c)
            )
    for via in RELAY:
        z_copies[via].wait_recv()
        for p, relay in LEAF.items():
            if relay == via:
                z_send(p, via)
    wait(feats.at[pl.ds(0, NP - 1)], a_ss)
    wait(part, p_ss)
    wait(bsend.at[pl.ds(0, NZ - 1)], b_ss)
    wait(dagg.at[pl.ds(0, NZ - 1)], c_ss)
    wait(dagg.at[pl.ds(0, NZ)], cs_ss)
    wait(erecv.at[pl.ds(1, 2 * NP - 1)], e_ss)

    for p in NEAR + list(LEAF):
        z_copies[p].wait_recv()
    acc = zall[0].astype(F32)
    for i in range(1, NZ):
        acc = acc + zall[i].astype(F32)
    fin[r, core] = acc
    for i, t in pairs:
        piece = fin.at[r, core, pl.ds(0, 8)] if i else fin.at[r, core]
        send(piece, piece, g_ss.at[0], g_rs.at[0], (plane(i), z * 2 + cores[t]))
    wait(zall.at[pl.ds(0, NZ - 1)], z_ss)

    acc = qpart[0].astype(F32)
    for i in FAR_FIRST:
        q_copies[i].wait_recv()
        acc = acc + qrecv[i].astype(F32)
    gf[...] = acc.astype(BF16)
    wait(fin.at[pl.ds(0, NP // 2)], g_rs)
    for h in range(2):
        lanes = slice(T * h, T * h + T)
        for p in range(NP):
            gw[8 * p : 8 * p + 8, lanes] = fin[p, h, 0:8]
        gb[:, lanes] = jnp.sum(fin[r, h, 8:16], axis=0, keepdims=True)
    wait(qrecv.at[pl.ds(0, NP - 1)], q_ss)
    wait(fin.at[pl.ds(0, NP // 2)], g_ss)


def write_out(*refs):
    sem = refs[-1]
    copies = [pltpu.make_async_copy(refs[n], refs[4 + n], sem.at[n]) for n in range(4)]
    for copy in copies:
        copy.start()
    for copy in copies:
        copy.wait()


def on_device(features, tiles, tile_rows, tile_cols, tile_count, weight, bias, cotangent):
    vmem = pl.BlockSpec(memory_space=pltpu.VMEM)
    hbm = pl.BlockSpec(memory_space=pl.ANY)
    dma = pltpu.SemaphoreType.DMA
    shapes = (
        jax.ShapeDtypeStruct((T, HID), BF16),
        jax.ShapeDtypeStruct((T, T), BF16),
        jax.ShapeDtypeStruct((T, HID), F32),
        jax.ShapeDtypeStruct((1, HID), F32),
    )
    results = pl.pallas_call(
        kernel,
        out_shape=shapes,
        in_specs=[hbm] * 8,
        out_specs=(vmem,) * 4,
        scratch_shapes=[
            pltpu.SMEM((K,), jnp.int32),
            pltpu.SMEM((K,), jnp.int32),
            pltpu.SMEM((1,), jnp.int32),
            pltpu.VMEM((K, T, T), BF16),
            pltpu.VMEM((T, HID), F32),
            pltpu.VMEM((1, HID), F32),
            pltpu.VMEM((T, HID), BF16),
            pltpu.VMEM((NP, T, T), BF16),
            pltpu.VMEM((K + 1, T, T), F32),
            pltpu.VMEM((NZ, T, T), BF16),
            pltpu.VMEM((NZ, T, T), BF16),
            pltpu.VMEM((2, T, HID), BF16),
            pltpu.VMEM((NZ, T, T), BF16),
            pltpu.VMEM((NZ, T, T), BF16),
            pltpu.VMEM((2 * NZ, T, T), BF16),
            pltpu.VMEM((NP, T, T), BF16),
            pltpu.VMEM((NP, T, T), BF16),
            pltpu.VMEM((NP, 2, 16, T), BF16),
            pltpu.VMEM((2 * NP, 16, T), BF16),
            pltpu.VMEM((NZ, 16, T), BF16),
            pltpu.VMEM((NP, 2, 16, T), F32),
        ]
        + [dma((n,)) for n in (8, 1, 1, 1, 4, 1, 20, 1, 30, 1, 1, 1, 16, 1, 1, 1, 15, 1, 1)],
        compiler_params=pltpu.CompilerParams(
            collective_id=0, has_side_effects=True, vmem_limit_bytes=60 * 1024 * 1024
        ),
    )(
        features,
        tiles.reshape(K, T, T),
        tile_rows.reshape(K),
        tile_cols.reshape(K),
        tile_count.reshape(1),
        weight,
        bias.reshape(1, HID),
        cotangent,
    )
    out, gf, gw, gb = pl.pallas_call(
        write_out,
        out_shape=shapes,
        in_specs=[vmem] * 4,
        out_specs=(hbm,) * 4,
        scratch_shapes=[dma((4,))],
    )(*results)
    return out, gf, gw, gb.reshape(HID)


def solution(mesh):
    placed = (
        P(("col", "row"), None),
        P("row", "col", None, None, None),
        P("row", "col", None),
        P("row", "col", None),
        P("row", "col"),
        P(),
        P(),
        P(("row", "col"), None),
    )
    return jax.shard_map(
        on_device,
        mesh=mesh,
        in_specs=placed,
        out_specs=(P(("row", "col"), None), P(("col", "row"), None), P(), P()),
        check_vma=False,
    )
```

```python
import jax
import jax.numpy as jnp
from jax import lax
from jax.experimental import pallas as pl
from jax.experimental.pallas import tpu as pltpu
from jax.sharding import PartitionSpec as P

MESH = pl.DeviceIdType.MESH
F32 = jnp.float32
BF16 = jnp.bfloat16
T = 128
K = 16
NX = 4
NY = 4
NZ = 16
NP = NX * NY
BR = 32
NODES = 65536
HID = 256
LEAF = {8: 5, 7: 5, 6: 5, 4: 5, -7: -5, -6: -5, -4: -5, 3: 2, -3: -2}
RELAY = [5, -5, 2, -2]
NEAR = [1, -1]
ORDER = list(LEAF) + NEAR + RELAY + [0]
FAR_FIRST = sorted(range(1, NP), key=lambda i: -min(i // 4, 4 - i // 4) - min(i % 4, 4 - i % 4))
AT = {p: n for n, p in enumerate(ORDER)}
ZNEAR = [1, 2, 3, 5, 11, 13, 14, 15]
C0 = 0.7978845608028654
C1 = 0.044715


def dot(a, b, dims=((1,), (0,))):
    return lax.dot_general(a, b, (dims, ((), ())), preferred_element_type=F32)


def split(v):
    hi = v.astype(BF16)
    return hi, (v - hi.astype(F32)).astype(BF16)


def kernel(
    feat, tiles_hbm, rows_hbm, cols_hbm, count_hbm, w_hbm, bias_hbm, cot_hbm,
    out, gf, gw, gb,
    rows, cols, count, tiles, w, bias, cot, feats, sums, part, sib, wsplit, bsend, brecv, dagg, qpart, qrecv,
    epart, erecv, zall, fin,
    in_sem, a_ss, a_rs, p_ss, p_rs, b_ss, b_rs,
    c_ss, c_rs, cs_ss, cs_rs, q_ss, q_rs,
    e_ss, e_rs, z_ss, z_rs, g_ss, g_rs,
):
    r = lax.axis_index("row")
    c = lax.axis_index("col")
    y, x = r // NX, r % NX
    z, core = c // 2, c % 2

    def plane(i):
        return ((y + i // NX) % NY) * NX + (x + i % NX) % NX

    def ring(i):
        return ((z + i) % NZ) * 2 + core

    me_other = (r, z * 2 + 1 - core)
    operands = (
        (feat, feats.at[r]), (rows_hbm, rows), (cols_hbm, cols), (count_hbm, count),
        (tiles_hbm, tiles), (w_hbm, w), (bias_hbm, bias), (cot_hbm, cot),
    )
    loads = [pltpu.make_async_copy(a, b, in_sem.at[n]) for n, (a, b) in enumerate(operands)]
    for copy in loads:
        copy.start()
    def send(src, dst, ssem, rsem, where):
        copy = pltpu.make_async_remote_copy(
            src_ref=src, dst_ref=dst, send_sem=ssem, recv_sem=rsem,
            device_id=where, device_id_type=MESH,
        )
        copy.start()
        return copy

    def wait(ref, sem):
        pltpu.make_async_copy(ref, ref, sem.at[0]).wait()

    barrier = pltpu.get_barrier_semaphore()
    for i in range(1, NP):
        pl.semaphore_signal(barrier, inc=1, device_id=(plane(i), c), device_id_type=MESH)
    for i in ZNEAR:
        pl.semaphore_signal(barrier, inc=1, device_id=(r, ring(i)), device_id_type=MESH)
    pl.semaphore_signal(barrier, inc=1, device_id=me_other, device_id_type=MESH)
    pl.semaphore_wait(barrier, NP + len(ZNEAR))

    for i in FAR_FIRST:
        send(feat, feats.at[r], a_ss.at[0], a_rs.at[0], (plane(i), c))

    for copy in loads[1:4]:
        copy.wait()
    live = count[0]
    dead = [NODES * jnp.minimum(jnp.maximum(k + 1 - live, 0), 1) for k in range(K)]
    slot_r = [rows[k] + dead[k] for k in range(K)]
    slot_c = [cols[k] + dead[k] for k in range(K)]

    def latest(slots, n, b):
        found = jnp.int32(0)
        for k in range(n):
            apart = slots[k] - b
            differs = jnp.minimum(jnp.maximum(apart, -apart), 1)
            found = jnp.maximum(found, (k + 1) * (1 - differs))
        return found

    prev_r = [latest(slot_r, k, slot_r[k]) for k in range(K)]
    prev_c = [latest(slot_c, k, slot_c[k]) for k in range(K)]
    last_r = [
        [latest(slot_r, K, ring(NZ - p) // 2 * 2 + half) for p in ORDER]
        for half in (1 - core, core)
    ]
    last_c = [latest(slot_c, K, plane(i)) for i in range(NP)]

    sums[0] = jnp.zeros((T, T), F32)
    for copy in (loads[0], *loads[4:]):
        copy.wait()
    wait(feats.at[pl.ds(0, NP - 1)], a_rs)

    for k in range(K):
        sums[k + 1] = dot(tiles[k], feats[jnp.minimum(jnp.maximum(cols[k], 0), NP - 1)])
    for k in range(1, K):
        sums[k + 1] = sums[k + 1] + sums[prev_r[k]]

    p_copies = []
    for g in range(4):
        for j in range(4 * g, 4 * g + 4):
            part[j] = sums[last_r[0][j]].astype(BF16)
        four = pl.ds(4 * g, 4)
        p_copies.append(
            send(part.at[four], sib.at[four], p_ss.at[0], p_rs.at[g], me_other)
        )

    halves = (pl.ds(0, T // 2), pl.ds(T // 2, T // 2))
    signs = (1, -1)
    b_copies = {}
    waited = set()

    def own(h, p):
        j = AT[(signs[h] * p + 7) % NZ - 7]
        if j // 4 not in waited:
            p_copies[j // 4].wait_recv()
            waited.add(j // 4)
        return sums[last_r[1][j], halves[h]] + sib[j, halves[h]].astype(F32)

    def pass_on(h, p, to):
        v = own(h, p)
        leaves = [AT[leaf] for leaf, relay in LEAF.items() if relay == p]
        if leaves:
            held = brecv.at[pl.ds(leaves[0], len(leaves)), halves[h]]
            pltpu.make_async_copy(held, held, b_rs.at[10 * h + RELAY.index(p)]).wait()
        for n in leaves:
            v = v + brecv[n, halves[h]].astype(F32)
        n = AT[p]
        bsend[n, halves[h]] = v.astype(BF16)
        b_copies[h, p] = send(
            bsend.at[n, halves[h]], brecv.at[n, halves[h]], b_ss.at[0],
            b_rs.at[10 * h + (RELAY.index(to) if to else n - len(LEAF) + 4)],
            (r, ring(NZ + signs[h] * (to - p))),
        )

    for h in range(2):
        for p in list(LEAF) + NEAR:
            pass_on(h, p, LEAF.get(p, 0))
    w_hi, w_lo = split(w[...])
    wsplit[0] = w_hi
    wsplit[1] = w_lo
    for h in range(2):
        for p in RELAY:
            pass_on(h, p, 0)

    c_copies = {}

    def c_send(h, p, via):
        block = dagg.at[ring(NZ - signs[h] * via), halves[h]]
        c_copies[h, p] = send(
            block, block, c_ss.at[0], c_rs.at[15 * h + AT[p]], (r, ring(NZ + signs[h] * (p - via)))
        )

    def c_share(h, p):
        block = dagg.at[ring(NZ - signs[h] * p), halves[h]]
        send(block, block, cs_ss.at[0], cs_rs.at[0], me_other)

    back, down0 = ((1,), (1,)), ((0,), (0,))
    kept = []
    for h in range(2):
        total = own(h, 0)
        for p in NEAR + RELAY:
            b_copies[h, p].wait_recv()
            total = total + brecv[AT[p], halves[h]].astype(F32)
        agg = total.astype(BF16)
        w_hi, w_lo = wsplit[0], wsplit[1]
        pre = dot(agg, w_hi) + dot(agg, w_lo) + bias[...]
        square = pre * pre
        t = jnp.tanh(C0 * (pre + C1 * (square * pre)))
        half = 0.5 * (1.0 + t)
        slope = half + 0.5 * pre * (1.0 - t * t) * (C0 * (1.0 + 3.0 * C1 * square))
        dpre = cot[halves[h], :].astype(F32) * slope
        dp_hi, dp_lo = split(dpre)
        da = dot(dp_hi, w_hi, back) + dot(dp_lo, w_hi, back) + dot(dp_hi, w_lo, back)
        dagg[c, halves[h]] = da.astype(BF16)
        for p in RELAY + NEAR:
            c_send(h, p, 0)
        c_share(h, 0)
        out[halves[h], :] = (pre * half).astype(BF16)
        kept.append((agg, dp_hi, dp_lo, dpre))

    local_w = local_b = 0.0
    for agg, dp_hi, dp_lo, dpre in kept:
        local_w = local_w + dot(agg, dp_hi, down0) + dot(agg, dp_lo, down0)
        local_b = local_b + jnp.sum(dpre.reshape(T // 16, 8, HID), axis=0)
    for h in range(2):
        lanes = slice(T * h, T * h + T)
        for p in range(NP):
            piece = (local_w[8 * p : 8 * p + 8, lanes], local_b[:, lanes])
            epart[p, h] = jnp.concatenate(piece, axis=0).astype(BF16)

    cores = (core, 1 - core)
    pairs = [(i, t) for i in FAR_FIRST + [0] for t in (0, 1) if i or t]
    for i, t in pairs:
        send(
            epart.at[plane(i), cores[t]], erecv.at[2 * i + t], e_ss.at[0], e_rs.at[0],
            (plane(i), z * 2 + cores[t]),
        )

    for h in range(2):
        for via in RELAY:
            c_copies[h, via].wait_recv()
            for p, relay in LEAF.items():
                if relay == via:
                    c_send(h, p, via)
            c_share(h, via)
        for p in NEAR:
            c_copies[h, p].wait_recv()
            c_share(h, p)

    z_copies = {}

    def z_send(p, via):
        slot = zall.at[(z + NZ - via) % NZ]
        z_copies[p] = send(
            slot, slot, z_ss.at[0], z_rs.at[AT[p]], (r, ring(NZ + p - via))
        )

    for turn, (h, p) in enumerate((h, p) for h in range(2) for p in LEAF):
        c_copies[h, p].wait_recv()
        c_share(h, p)
        if turn == 5:
            wait(erecv.at[pl.ds(1, 2 * NP - 1)], e_rs)
            acc = epart[r, core].astype(F32)
            for n in range(1, 2 * NP):
                acc = acc + erecv[n].astype(F32)
            zall[z] = acc.astype(BF16)
            for p in RELAY + NEAR:
                z_send(p, 0)

    wait(dagg.at[pl.ds(0, NZ)], cs_rs)

    for k in range(K):
        picked = dagg[jnp.minimum(jnp.maximum(rows[k], 0), BR - 1)]
        sums[k + 1] = dot(tiles[k], picked, down0)
    for k in range(1, K):
        sums[k + 1] = sums[k + 1] + sums[prev_c[k]]
    q_copies = {}
    for i in FAR_FIRST + [0]:
        qpart[i] = sums[last_c[i]].astype(BF16)
        if i:
            q_copies[i] = send(
                qpart.at[i], qrecv.at[i], q_ss.at[0], q_rs.at[i], (plane(i), c)
            )
    for via in RELAY:
        z_copies[via].wait_recv()
        for p, relay in LEAF.items():
            if relay == via:
                z_send(p, via)
    wait(feats.at[pl.ds(0, NP - 1)], a_ss)
    wait(part, p_ss)
    wait(bsend.at[pl.ds(0, NZ - 1)], b_ss)
    wait(dagg.at[pl.ds(0, NZ - 1)], c_ss)
    wait(dagg.at[pl.ds(0, NZ)], cs_ss)
    wait(erecv.at[pl.ds(1, 2 * NP - 1)], e_ss)

    for p in NEAR + list(LEAF):
        z_copies[p].wait_recv()
    acc = zall[0].astype(F32)
    for i in range(1, NZ):
        acc = acc + zall[i].astype(F32)
    fin[r, core] = acc
    for i, t in pairs:
        piece = fin.at[r, core, pl.ds(0, 8)] if i else fin.at[r, core]
        send(piece, piece, g_ss.at[0], g_rs.at[0], (plane(i), z * 2 + cores[t]))
    wait(zall.at[pl.ds(0, NZ - 1)], z_ss)

    acc = qpart[0].astype(F32)
    for i in FAR_FIRST:
        q_copies[i].wait_recv()
        acc = acc + qrecv[i].astype(F32)
    gf[...] = acc.astype(BF16)
    wait(fin.at[pl.ds(0, NP // 2)], g_rs)
    for h in range(2):
        lanes = slice(T * h, T * h + T)
        for p in range(NP):
            gw[8 * p : 8 * p + 8, lanes] = fin[p, h, 0:8]
        gb[:, lanes] = jnp.sum(fin[r, h, 8:16], axis=0, keepdims=True)
    wait(qrecv.at[pl.ds(0, NP - 1)], q_ss)
    wait(fin.at[pl.ds(0, NP // 2)], g_ss)


def write_out(*refs):
    sem = refs[-1]
    copies = [pltpu.make_async_copy(refs[n], refs[4 + n], sem.at[n]) for n in range(4)]
    for copy in copies:
        copy.start()
    for copy in copies:
        copy.wait()


def on_device(features, tiles, tile_rows, tile_cols, tile_count, weight, bias, cotangent):
    vmem = pl.BlockSpec(memory_space=pltpu.VMEM)
    hbm = pl.BlockSpec(memory_space=pl.ANY)
    dma = pltpu.SemaphoreType.DMA
    shapes = (
        jax.ShapeDtypeStruct((T, HID), BF16),
        jax.ShapeDtypeStruct((T, T), BF16),
        jax.ShapeDtypeStruct((T, HID), F32),
        jax.ShapeDtypeStruct((1, HID), F32),
    )
    results = pl.pallas_call(
        kernel,
        out_shape=shapes,
        in_specs=[hbm] * 8,
        out_specs=(vmem,) * 4,
        scratch_shapes=[
            pltpu.SMEM((K,), jnp.int32),
            pltpu.SMEM((K,), jnp.int32),
            pltpu.SMEM((1,), jnp.int32),
            pltpu.VMEM((K, T, T), BF16),
            pltpu.VMEM((T, HID), F32),
            pltpu.VMEM((1, HID), F32),
            pltpu.VMEM((T, HID), BF16),
            pltpu.VMEM((NP, T, T), BF16),
            pltpu.VMEM((K + 1, T, T), F32),
            pltpu.VMEM((NZ, T, T), BF16),
            pltpu.VMEM((NZ, T, T), BF16),
            pltpu.VMEM((2, T, HID), BF16),
            pltpu.VMEM((NZ, T, T), BF16),
            pltpu.VMEM((NZ, T, T), BF16),
            pltpu.VMEM((2 * NZ, T, T), BF16),
            pltpu.VMEM((NP, T, T), BF16),
            pltpu.VMEM((NP, T, T), BF16),
            pltpu.VMEM((NP, 2, 16, T), BF16),
            pltpu.VMEM((2 * NP, 16, T), BF16),
            pltpu.VMEM((NZ, 16, T), BF16),
            pltpu.VMEM((NP, 2, 16, T), F32),
        ]
        + [dma((n,)) for n in (8, 1, 1, 1, 4, 1, 20, 1, 30, 1, 1, 1, 16, 1, 1, 1, 15, 1, 1)],
        compiler_params=pltpu.CompilerParams(
            collective_id=0, has_side_effects=True, vmem_limit_bytes=60 * 1024 * 1024
        ),
    )(
        features,
        tiles.reshape(K, T, T),
        tile_rows.reshape(K),
        tile_cols.reshape(K),
        tile_count.reshape(1),
        weight,
        bias.reshape(1, HID),
        cotangent,
    )
    out, gf, gw, gb = pl.pallas_call(
        write_out,
        out_shape=shapes,
        in_specs=[vmem] * 4,
        out_specs=(hbm,) * 4,
        scratch_shapes=[dma((4,))],
    )(*results)
    return out, gf, gw, gb.reshape(HID)


def solution(mesh):
    placed = (
        P(("col", "row"), None),
        P("row", "col", None, None, None),
        P("row", "col", None),
        P("row", "col", None),
        P("row", "col"),
        P(),
        P(),
        P(("row", "col"), None),
    )
    return jax.shard_map(
        on_device,
        mesh=mesh,
        in_specs=placed,
        out_specs=(P(("row", "col"), None), P(("col", "row"), None), P(), P()),
        check_vma=False,
    )
```
